32 devices in a mesh: seq: 8 (over y, x, core), ch: 4 (over z).
Axes of the slice: x: 2, y: 2, z: 4, core: 2. Of those that a mesh axis runs over, the one named last changes fastest.
Arguments:
- tokens: bfloat16 [65536, 1024], P('seq', 'ch'), may hold values from -6 to 6
- gating: bfloat16 [65536, 1024], P('seq', 'ch'), may hold values from -6 to 6
- spectral_gain: float32 [32, 128, 1024], P(None, None, 'ch'), may hold values from 0.25 to 4
- device_gain: float32 [8, 1024], P(None, 'ch'), may hold values from 0.25 to 4
- retained: int32 [64], P('ch'), may hold values from 32 to 128, as said below
- block_weight: bfloat16 [4, 256, 256], replicated, may hold values from -0.375 to 0.375
- mix_weight: float32 [256, 4, 4], replicated, may hold values from -3 to 3
Outputs:
- channel_mixed: bfloat16 [65536, 1024], P(('seq', 'ch'))
The draws below stay inside these ranges and needn't reach their ends.
Inputs may be any that keep to these rules, and one draw needn't show every extreme that they name: `retained`: in every aligned run of 8 channel groups at least one group has 128, the most, at a position drawn from the seed; the others lie between 32 and 128.
All inputs are finite; a program needn't handle non-finite values.
Results may differ from the reference program's by a relative error of at most 0.0049.
Values may be sent and summed in bfloat16 or wider, within the bound.
A program may use at most 128 MiB of HBM per device.

```python
import math
import jax
import jax.numpy as jnp
from jax import lax

C = 1024
BLK = 256
GSZ = 16
B = 256
A = 32
KMAX = 128
NB = 4
LENGTH = 65536
N_SEQ = 8


def draw_retained(key, part):
    key = jax.random.fold_in(key, 7)
    first_key, second_key = jax.random.split(key)
    groups = C // GSZ
    base = jax.random.randint(first_key, (groups,), KMAX // 4, KMAX + 1)
    picked = jax.random.randint(second_key, (groups // 8,), 0, 8)
    chosen = jnp.arange(groups) % 8 == jnp.repeat(picked, 8)
    return jnp.where(chosen, KMAX, base).astype(jnp.int32)


def block_levels(rng, dims, cuts, smallest, top_value):
    gain = 1.0
    for dim, blocks in cuts:
        heights = jax.random.uniform(jax.random.fold_in(jax.random.fold_in(rng, 6), dim), (blocks,), jnp.float32, smallest / len(cuts), top_value / len(cuts))
        gain = gain * jnp.repeat(jnp.exp(heights), dims[dim] // blocks).reshape((-1,) + (1,) * (len(dims) - 1 - dim))
    return gain


def normal_values(own_key, dims, spread, bound, cuts=(), kind=jnp.bfloat16):
    values = jax.random.normal(own_key, dims, jnp.float32) * spread
    if len(cuts) > 0:
        values = block_levels(own_key, dims, cuts, -0.22, 0.18) * values
    return jnp.clip(values, min=-bound, max=bound).astype(kind)


def setup_inputs(seed: int = 0) -> dict:
    keys = jax.random.split(jax.random.key(seed), 8)
    return {
        "tokens": normal_values(keys[0], (LENGTH, C), 1.0, 6.0, ((0, 8), (1, 4))),
        "gating": normal_values(keys[1], (LENGTH, C), 1.0, 6.0, ((0, 8), (1, 4))),
        "spectral_gain": jnp.clip(jnp.exp(math.log(4.0) - 2.7725887 * jax.random.uniform(keys[2], (A, KMAX, C), jnp.float32) ** block_levels(keys[2], (A, KMAX, C), ((2, 4),), -0.2, 0.2)), 0.25, 4.0),
        "device_gain": jnp.clip(jnp.exp(math.log(4.0) - 2.7725887 * jax.random.uniform(keys[3], (N_SEQ, C), jnp.float32) ** block_levels(keys[3], (N_SEQ, C), ((1, 4),), -0.2, 0.2)), 0.25, 4.0),
        "retained": draw_retained(jax.random.fold_in(keys[7], 71), 0),
        "block_weight": normal_values(keys[5], (NB, BLK, BLK), BLK ** -0.5, 0.375),
        "mix_weight": normal_values(keys[6], (BLK, NB, NB), NB ** -0.5, 3.0, (), jnp.float32),
    }


def cosine_table(length):
    rows = jnp.arange(length, dtype=jnp.int32)[:, None].astype(jnp.float32)
    cols = jnp.arange(length, dtype=jnp.int32)[None, :].astype(jnp.float32)
    table = jnp.cos(math.pi * (2.0 * cols + 1.0) * rows / (2.0 * length)) * math.sqrt(2.0 / length)
    return jnp.where(rows == 0.0, table * math.sqrt(0.5), table)

def butterfly_table(devices):
    levels = devices.bit_length() - 1
    index = jnp.arange(devices, dtype=jnp.int32)
    table = jnp.ones((devices, devices), jnp.float32)
    for level in range(levels):
        angle = 0.6 + 0.1 * level
        row_bit = jnp.right_shift(index, level)[:, None] % 2
        col_bit = jnp.right_shift(index, level)[None, :] % 2
        same = jnp.where(row_bit == 0, math.cos(angle), -math.cos(angle))
        table = table * jnp.where(row_bit == col_bit, same, math.sin(angle)).astype(jnp.float32)
    return table

def reference(tokens, gating, spectral_gain, device_gain, retained, block_weight, mix_weight):
    high = lax.Precision.HIGHEST
    width = 128
    band_table = cosine_table(B)[:KMAX]
    block_table = cosine_table(A)
    outer_table = butterfly_table(N_SEQ)
    group_keep = jnp.repeat(retained, GSZ)

    def seq_block(block):
        start = block * width
        columns = lax.dynamic_slice_in_dim(tokens, start, width, 1).astype(jnp.float32).reshape(N_SEQ, A, B, width)
        gains = lax.dynamic_slice_in_dim(spectral_gain, start, width, 2)
        keeps = lax.dynamic_slice_in_dim(group_keep, start, width, 0)
        passband = jnp.arange(KMAX, dtype=jnp.int32)[:, None] < keeps[None, :]
        row_gain = lax.dynamic_slice_in_dim(device_gain, start, width, 1)
        spectra = jnp.einsum('kb,pabc->pakc', band_table, columns, precision=high)
        spectra = jnp.einsum('ja,pakc->pjkc', block_table, spectra, precision=high)
        spectra = spectra * jnp.where(passband, gains, 0.0)[None]
        spectra = jnp.einsum('qp,pjkc->qjkc', outer_table, spectra, precision=high)
        spectra = spectra * row_gain[:, None, None, :]
        spectra = jnp.einsum('rq,qjkc->rjkc', outer_table, spectra, precision=high)
        spectra = jnp.einsum('ja,pjkc->pakc', block_table, spectra, precision=high)
        spectra = jnp.einsum('kb,pakc->pabc', band_table, spectra, precision=high)
        gate_cols = lax.dynamic_slice_in_dim(gating, start, width, 1).astype(jnp.float32)
        return (gate_cols * spectra.reshape(LENGTH, width)).astype(jnp.bfloat16)
    gated = lax.map(seq_block, jnp.arange(C // width, dtype=jnp.int32))
    gated = jnp.transpose(gated, (1, 0, 2)).reshape(LENGTH, C)
    row_block = min(LENGTH, 4096)
    weight_f = block_weight.astype(jnp.float32)

    def mix_rows(block):
        rows = lax.dynamic_slice_in_dim(gated, block * row_block, row_block, 0).astype(jnp.float32)
        rows = rows.reshape(row_block, NB, BLK)
        first_section = jnp.einsum('rid,ide->rie', rows, weight_f, precision=high)
        result = jnp.einsum('rie,eki->rke', first_section, mix_weight, precision=high)
        return result.reshape(row_block, C).astype(jnp.bfloat16)
    mixed = lax.map(mix_rows, jnp.arange(LENGTH // row_block, dtype=jnp.int32))
    return mixed.reshape(LENGTH, C)
```

```python
import functools
import math

import jax
import jax.numpy as jnp
import ml_dtypes
import numpy as np
from jax import lax
from jax.experimental import pallas as pl
from jax.experimental.pallas import tpu as pltpu
from jax.sharding import PartitionSpec as P

GSZ = 16
B = 256
A = 32
KMAX = 128
LANES = 128
MESH = pl.DeviceIdType.MESH
F32 = jnp.float32
BF16 = jnp.bfloat16


def cosine_table(length):
    rows = np.arange(length, dtype=np.float64)[:, None]
    cols = np.arange(length, dtype=np.float64)[None, :]
    table = np.cos(math.pi * (2.0 * cols + 1.0) * rows / (2.0 * length)) * math.sqrt(2.0 / length)
    return np.where(rows == 0.0, table * math.sqrt(0.5), table)


def split(table):
    high = table.astype(ml_dtypes.bfloat16)
    low = (table - high.astype(np.float64)).astype(ml_dtypes.bfloat16)
    return high, low


def tables():
    band_high, band_low = split(cosine_table(B)[:KMAX])
    mid_high, mid_low = split(np.kron(cosine_table(A), np.eye(8)))
    back_high, back_low = split(np.kron(cosine_table(A).T, np.eye(8)))
    return (
        np.concatenate([band_high, band_low], 0),
        np.concatenate([mid_high, mid_low, mid_high], 1),
        np.concatenate([back_high, back_low], 1),
        np.concatenate([band_high.T, band_low.T, band_high.T], 1),
    )


def dot(left, right):
    return jnp.dot(left, right, preferred_element_type=F32)


def two_parts(value):
    high = value.astype(BF16)
    return high, (value - high.astype(F32)).astype(BF16)


def butterfly(parts, levels):
    for level in range(levels):
        angle = 0.6 + 0.1 * level
        cos, sin = math.cos(angle), math.sin(angle)
        mixed = list(parts)
        for low in range(len(parts)):
            if (low >> level) % 2 == 0:
                high = low + (1 << level)
                mixed[low] = cos * parts[low] + sin * parts[high]
                mixed[high] = sin * parts[low] - cos * parts[high]
        parts = mixed
    return parts


def filter_kernel(n, nc, halves, tok, gate, gain, dgain, keep, band, mid, back, inner, out,
                  xt, gt, gn, z, snd, rcv, mxo, bck, gsd,
                  xsem, gsem, nsem, s1, r1, s2, r2, s3, r3, own3):
    me = lax.axis_index("seq")
    mc = lax.axis_index("ch")
    levels = n.bit_length() - 1
    jn = A // n
    an = A // nc

    def cut(h):
        return pl.ds(h * LANES, LANES)

    loads = {}
    for h in range(halves):
        loads["x", h] = pltpu.make_async_copy(tok.at[:, :, cut(h)], xt.at[h], xsem.at[h])
        loads["n", h] = pltpu.make_async_copy(gain.at[:, :, cut(h)], gn.at[h], nsem.at[h])
        loads["g", h] = pltpu.make_async_copy(gate.at[:, :, cut(h)], gt.at[h], gsem.at[h])
    for name in ("x", "n"):
        loads[name, 0].start()
    for h in range(1, halves):
        loads["x", h].start()
        loads["n", h].start()
    for h in range(halves):
        loads["g", h].start()

    barrier = pltpu.get_barrier_semaphore()
    for s in range(1, n):
        pl.semaphore_signal(barrier, inc=1, device_id={"seq": lax.rem(me + s, n)}, device_id_type=MESH)
    for s in range(1, nc):
        pl.semaphore_signal(barrier, inc=1, device_id={"ch": lax.rem(mc + s, nc)}, device_id_type=MESH)

    def forward(h):
        loads["x", h].wait()

        def first(a, carry):
            both = dot(band[...], xt[h, a])
            z[a] = both[:KMAX] + both[KMAX:]
            return carry

        lax.fori_loop(0, A, first, 0, unroll=4)
        loads["n", h].wait()
        keeps = keep[:, h * LANES:(h + 1) * LANES].reshape(1, 1, LANES)

        def second(kb, carry):
            start = pl.multiple_of(kb * 16, 16)
            block = z[:, pl.ds(start, 16), :]
            pieces = []
            for part in range(2):
                value = block[:, part * 8:part * 8 + 8].reshape(A * 8, LANES)
                high, low = two_parts(value)
                pieces.append(dot(mid[...], jnp.concatenate([high, high, low], 0)).reshape(A, 8, LANES))
            value = jnp.concatenate(pieces, 1)
            index = start + lax.broadcasted_iota(jnp.int32, (1, 16, LANES), 1)
            value = value * jnp.where(index < keeps, gn[h, :, pl.ds(start, 16), :], 0.0)
            snd[h, :, :, pl.ds(start, 16), :] = value.astype(BF16).reshape(n, jn, 16, LANES)
            return carry

        lax.fori_loop(0, KMAX // 16, second, 0)

    def exchange(src, dst, ssem, rsem, h):
        copies = []
        for s in range(1, n):
            to = lax.rem(me + s, n)
            copies.append(pltpu.make_async_remote_copy(
                src_ref=src.at[h, to], dst_ref=dst.at[h, me],
                send_sem=ssem.at[h, s], recv_sem=rsem.at[h, s],
                device_id={"seq": to}, device_id_type=MESH))
        return copies

    def mix(h):
        rcv[h, me] = snd[h, me]
        rows = [dgain[r:r + 1, h * LANES:(h + 1) * LANES] for r in range(n)]

        def step(i, carry):
            j = i // (KMAX // 16)
            start = pl.multiple_of(lax.rem(i, KMAX // 16) * 16, 16)
            parts = [rcv[h, p, j, pl.ds(start, 16), :].astype(F32) for p in range(n)]
            parts = butterfly(parts, levels)
            parts = [part * row for part, row in zip(parts, rows)]
            parts = butterfly(parts, levels)
            for q in range(n):
                mxo[h, q, j, pl.ds(start, 16), :] = parts[q].astype(BF16)
            return carry

        lax.fori_loop(0, jn * (KMAX // 16), step, 0)
        bck[h, me] = mxo[h, me]

    def inverse_mid(h):
        def step(kb, carry):
            start = pl.multiple_of(kb * 16, 16)
            block = bck[h, :, :, pl.ds(start, 16), :].reshape(A, 16, LANES).astype(F32)
            for part in range(2):
                value = block[:, part * 8:part * 8 + 8].reshape(A * 8, LANES).astype(BF16)
                value = dot(back[...], jnp.concatenate([value, value], 0))
                z[:, pl.ds(start + part * 8, 8), :] = value.reshape(A, 8, LANES)
            return carry

        lax.fori_loop(0, KMAX // 16, step, 0)

    def inverse_rows(h, to):
        def step(i, carry):
            a = to * an + i
            high, low = two_parts(z[a])
            smooth = dot(inner[...], jnp.concatenate([high, high, low], 0))
            gsd[h, a] = (smooth * gt[h, a].astype(F32)).astype(BF16)
            return carry

        lax.fori_loop(0, an, step, 0, unroll=2)

    def run(copies):
        for copy in copies:
            copy.start()

    first = [exchange(snd, rcv, s1, r1, h) for h in range(halves)]
    second = [exchange(mxo, bck, s2, r2, h) for h in range(halves)]
    third = []

    def finish(h):
        for copy in second[h]:
            copy.wait_recv()
        inverse_mid(h)
        loads["g", h].wait()
        for s in list(range(nc // 2, 0, -1)) + list(range(nc // 2 + 1, nc)):
            to = lax.rem(mc + s, nc)
            inverse_rows(h, to)
            copy = pltpu.make_async_remote_copy(
                src_ref=gsd.at[h, pl.ds(to * an, an)], dst_ref=out.at[h, mc],
                send_sem=s3.at[h, s], recv_sem=r3.at[h, s],
                device_id={"ch": to}, device_id_type=MESH)
            copy.start()
            third.append(copy)
        inverse_rows(h, mc)
        copy = pltpu.make_async_copy(gsd.at[h, pl.ds(mc * an, an)], out.at[h, mc], own3.at[h])
        copy.start()
        third.append(copy)

    forward(0)
    pl.semaphore_wait(barrier, n - 1 + nc - 1)
    run(first[0])
    for h in range(halves):
        if h + 1 < halves:
            forward(h + 1)
        for copy in first[h]:
            copy.wait_recv()
        mix(h)
        run(second[h])
        if h + 1 < halves:
            run(first[h + 1])
        finish(h)
    for copy in third:
        copy.wait()
    for copies in first + second:
        for copy in copies:
            copy.wait_send()


def mixing_kernel(nc, halves, nb, gathered, weight, mixing, out):
    size = weight.shape[1]
    per = size // LANES
    tiles = [gathered[h, c].reshape(-1, LANES) for c in range(nc) for h in range(halves)]
    sections = [
        dot(jnp.concatenate(tiles[i * per:(i + 1) * per], 1), weight[i]) for i in range(nb)
    ]
    for k in range(nb):
        total = sections[0] * mixing[k * nb:k * nb + 1]
        for i in range(1, nb):
            total += sections[i] * mixing[k * nb + i:k * nb + i + 1]
        out[:, k * size:(k + 1) * size] = total.astype(BF16)


def local(n, nc, tokens, gating, spectral_gain, device_gain, retained, block_weight, mix_weight):
    rows, width = tokens.shape
    halves = width // LANES
    an = A // nc
    jn = A // n
    keep = jnp.repeat(retained, GSZ)[None, :]
    any_space = pl.BlockSpec(memory_space=pl.ANY)
    vmem = pl.BlockSpec(memory_space=pltpu.VMEM)
    dma = pltpu.SemaphoreType.DMA
    share = (halves, n, jn, KMAX, LANES)
    gathered = pl.pallas_call(
        functools.partial(filter_kernel, n, nc, halves),
        out_shape=jax.ShapeDtypeStruct((halves, nc, an, B, LANES), BF16),
        in_specs=[any_space] * 3 + [vmem] * 6,
        out_specs=any_space,
        scratch_shapes=[
            pltpu.VMEM((halves, A, B, LANES), BF16),
            pltpu.VMEM((halves, A, B, LANES), BF16),
            pltpu.VMEM((halves, A, KMAX, LANES), F32),
            pltpu.VMEM((A, KMAX, LANES), F32),
            pltpu.VMEM(share, BF16),
            pltpu.VMEM(share, BF16),
            pltpu.VMEM(share, BF16),
            pltpu.VMEM(share, BF16),
            pltpu.VMEM((halves, A, B, LANES), BF16),
            dma((halves,)), dma((halves,)), dma((halves,)),
            dma((halves, n)), dma((halves, n)), dma((halves, n)), dma((halves, n)),
            dma((halves, nc)), dma((halves, nc)), dma((halves,)),
        ],
        compiler_params=pltpu.CompilerParams(
            collective_id=0, has_side_effects=True, vmem_limit_bytes=48 * 1024 * 1024),
        name="filter",
    )(tokens.reshape(A, B, width), gating.reshape(A, B, width), spectral_gain, device_gain, keep,
      *[jnp.asarray(table) for table in tables()])
    nb, size, _ = block_weight.shape
    mixing = jnp.transpose(mix_weight, (1, 2, 0)).reshape(nb * nb, size)
    step = 2 if an % 2 == 0 else 1
    return pl.pallas_call(
        functools.partial(mixing_kernel, nc, halves, nb),
        out_shape=jax.ShapeDtypeStruct((an * B, nb * size), BF16),
        grid=(an // step,),
        in_specs=[
            pl.BlockSpec((halves, nc, step, B, LANES), lambda i: (0, 0, i, 0, 0)),
            pl.BlockSpec(block_weight.shape, lambda i: (0, 0, 0)),
            pl.BlockSpec(mixing.shape, lambda i: (0, 0)),
        ],
        out_specs=pl.BlockSpec((step * B, nb * size), lambda i: (i, 0)),
        compiler_params=pltpu.CompilerParams(vmem_limit_bytes=40 * 1024 * 1024),
        name="mixing",
    )(gathered, block_weight, mixing)


def solution(mesh):
    in_specs = (
        P("seq", "ch"),
        P("seq", "ch"),
        P(None, None, "ch"),
        P(None, "ch"),
        P("ch"),
        P(),
        P(),
    )
    out_specs = P(("seq", "ch"), None)
    body = functools.partial(local, mesh.shape["seq"], mesh.shape["ch"])
    return jax.shard_map(body, mesh=mesh, in_specs=in_specs, out_specs=out_specs, check_vma=False)
```

```python
import functools
import math

import jax
import jax.numpy as jnp
import ml_dtypes
import numpy as np
from jax import lax
from jax.experimental import pallas as pl
from jax.experimental.pallas import tpu as pltpu
from jax.sharding import PartitionSpec as P

GSZ = 16
B = 256
A = 32
KMAX = 128
LANES = 128
MESH = pl.DeviceIdType.MESH
F32 = jnp.float32
BF16 = jnp.bfloat16


def cosine_table(length):
    rows = np.arange(length, dtype=np.float64)[:, None]
    cols = np.arange(length, dtype=np.float64)[None, :]
    table = np.cos(math.pi * (2.0 * cols + 1.0) * rows / (2.0 * length)) * math.sqrt(2.0 / length)
    return np.where(rows == 0.0, table * math.sqrt(0.5), table)


def split(table):
    high = table.astype(ml_dtypes.bfloat16)
    low = (table - high.astype(np.float64)).astype(ml_dtypes.bfloat16)
    return high, low


def tables():
    band_high, band_low = split(cosine_table(B)[:KMAX])
    mid_high, mid_low = split(np.kron(cosine_table(A), np.eye(8)))
    back_high, back_low = split(np.kron(cosine_table(A).T, np.eye(8)))
    return (
        np.concatenate([band_high, band_low], 0),
        np.concatenate([mid_high, mid_low, mid_high], 1),
        np.concatenate([back_high, back_low], 1),
        np.concatenate([band_high.T, band_low.T, band_high.T], 1),
    )


def dot(left, right):
    return jnp.dot(left, right, preferred_element_type=F32)


def two_parts(value):
    high = value.astype(BF16)
    return high, (value - high.astype(F32)).astype(BF16)


def butterfly(parts, levels):
    for level in range(levels):
        angle = 0.6 + 0.1 * level
        cos, sin = math.cos(angle), math.sin(angle)
        mixed = list(parts)
        for low in range(len(parts)):
            if (low >> level) % 2 == 0:
                high = low + (1 << level)
                mixed[low] = cos * parts[low] + sin * parts[high]
                mixed[high] = sin * parts[low] - cos * parts[high]
        parts = mixed
    return parts


def filter_kernel(n, nc, halves, early, tok, gate, gain, dgain, kept,
                  band_hbm, mid_hbm, back_hbm, inner_hbm, out,
                  xt, gt, gn, z, snd, rcv, mxo, bck, gsd, ysd, yrc, grc, ystage,
                  band, mid, back, inner, dg, retained, tsem,
                  xsem, gsem, nsem, s1, r1, s2, r2, s3, r3, own3, s4, r4, s5, r5, own5):
    me = lax.axis_index("seq")
    mc = lax.axis_index("ch")
    levels = n.bit_length() - 1
    jn = A // n
    an = A // nc

    def cut(h):
        return pl.ds(h * LANES, LANES)

    loads = {}
    for h in range(halves):
        loads["x", h] = pltpu.make_async_copy(tok.at[:, :, cut(h)], xt.at[h], xsem.at[h])
        loads["n", h] = pltpu.make_async_copy(gain.at[:, :, cut(h)], gn.at[h], nsem.at[h])
        loads["g", h] = pltpu.make_async_copy(gate.at[:, :, cut(h)], gt.at[h], gsem.at[h])
    for i, (src, dst) in enumerate((
            (band_hbm, band), (mid_hbm, mid), (dgain, dg), (back_hbm, back), (inner_hbm, inner),
            (kept, retained))):
        loads["t", i] = pltpu.make_async_copy(src, dst, tsem.at[i])
    loads["t", 5].start()
    loads["t", 0].start()
    loads["x", 0].start()
    loads["t", 1].start()
    loads["n", 0].start()
    for i in (2, 3, 4):
        loads["t", i].start()
    for h in range(1, halves):
        loads["x", h].start()
        loads["n", h].start()
    for h in range(halves):
        loads["g", h].start()

    barrier = pltpu.get_barrier_semaphore()
    for s in range(1, n):
        pl.semaphore_signal(barrier, inc=1, device_id={"seq": lax.rem(me + s, n)}, device_id_type=MESH)
    for s in range(1, nc):
        pl.semaphore_signal(barrier, inc=1, device_id={"ch": lax.rem(mc + s, nc)}, device_id_type=MESH)

    def forward(h):
        loads["x", h].wait()
        if h == 0:
            loads["t", 0].wait()

        def first(a, carry):
            both = dot(band[...], xt[h, a])
            z[a] = both[:KMAX] + both[KMAX:]
            return carry

        lax.fori_loop(0, A, first, 0, unroll=4)
        loads["n", h].wait()
        if h == 0:
            loads["t", 1].wait()
            loads["t", 5].wait()
        group = lax.broadcasted_iota(jnp.int32, (1, 1, LANES), 2) // GSZ
        keeps = jnp.zeros((1, 1, LANES), jnp.int32)
        for i in range(LANES // GSZ):
            keeps = jnp.where(group == i, retained[h * (LANES // GSZ) + i], keeps)

        def second(kb, carry):
            start = pl.multiple_of(kb * 16, 16)
            block = z[:, pl.ds(start, 16), :]
            pieces = []
            for part in range(2):
                value = block[:, part * 8:part * 8 + 8].reshape(A * 8, LANES)
                high, low = two_parts(value)
                pieces.append(dot(mid[...], jnp.concatenate([high, high, low], 0)).reshape(A, 8, LANES))
            value = jnp.concatenate(pieces, 1)
            index = start + lax.broadcasted_iota(jnp.int32, (1, 16, LANES), 1)
            value = value * jnp.where(index < keeps, gn[h, :, pl.ds(start, 16), :], 0.0)
            snd[h, :, :, pl.ds(start, 16), :] = value.astype(BF16).reshape(n, jn, 16, LANES)
            return carry

        lax.fori_loop(0, KMAX // 16, second, 0)

    def exchange(src, dst, ssem, rsem, h):
        copies = []
        for s in range(1, n):
            to = lax.rem(me + s, n)
            copies.append(pltpu.make_async_remote_copy(
                src_ref=src.at[h, to], dst_ref=dst.at[h, me],
                send_sem=ssem.at[h, s], recv_sem=rsem.at[h, s],
                device_id={"seq": to}, device_id_type=MESH))
        return copies

    def mix(h):
        rcv[h, me] = snd[h, me]
        if h == 0:
            for i in (2, 3, 4):
                loads["t", i].wait()
        rows = [dg[r:r + 1, h * LANES:(h + 1) * LANES] for r in range(n)]

        def step(i, carry):
            j = i // (KMAX // 16)
            start = pl.multiple_of(lax.rem(i, KMAX // 16) * 16, 16)
            parts = [rcv[h, p, j, pl.ds(start, 16), :].astype(F32) for p in range(n)]
            parts = butterfly(parts, levels)
            parts = [part * row for part, row in zip(parts, rows)]
            parts = butterfly(parts, levels)
            for q in range(n):
                mxo[h, q, j, pl.ds(start, 16), :] = parts[q].astype(BF16)
            return carry

        lax.fori_loop(0, jn * (KMAX // 16), step, 0)
        bck[h, me] = mxo[h, me]

    def inverse_mid(h):
        def step(kb, carry):
            start = pl.multiple_of(kb * 16, 16)
            block = bck[h, :, :, pl.ds(start, 16), :].reshape(A, 16, LANES).astype(F32)
            for part in range(2):
                value = block[:, part * 8:part * 8 + 8].reshape(A * 8, LANES).astype(BF16)
                value = dot(back[...], jnp.concatenate([value, value], 0))
                z[:, pl.ds(start + part * 8, 8), :] = value.reshape(A, 8, LANES)
            return carry

        lax.fori_loop(0, KMAX // 16, step, 0)

    def inverse_rows(h, to, skip):
        def step(i, carry):
            a = to * an + i
            high, low = two_parts(z[a])
            smooth = dot(inner[...], jnp.concatenate([high, high, low], 0))
            gsd[h, a] = (smooth * gt[h, a].astype(F32)).astype(BF16)
            return carry

        lax.fori_loop(skip, an, step, 0)

    def run(copies):
        for copy in copies:
            copy.start()

    first = [exchange(snd, rcv, s1, r1, h) for h in range(halves)]
    second = [exchange(mxo, bck, s2, r2, h) for h in range(halves)]
    third = []
    fourth = []
    order = list(range(nc // 2, 0, -1)) + list(range(nc // 2 + 1, nc))

    def finish(h):
        for copy in second[h]:
            copy.wait_recv()
        inverse_mid(h)
        loads["g", h].wait()
        skip = early if h == 0 else 0
        if h == 0:
            for s in order:
                to = lax.rem(mc + s, nc)
                ysd[pl.ds(to * early, early)] = z[pl.ds(to * an, early)].astype(BF16)
                copy = pltpu.make_async_remote_copy(
                    src_ref=ysd.at[pl.ds(to * early, early)], dst_ref=yrc.at[s],
                    send_sem=s5.at[s], recv_sem=r5.at[s],
                    device_id={"ch": to}, device_id_type=MESH)
                copy.start()
                fourth.append((s, copy))
        for s in order:
            to = lax.rem(mc + s, nc)
            inverse_rows(h, to, skip)
            copy = pltpu.make_async_remote_copy(
                src_ref=gsd.at[h, pl.ds(to * an + skip, an - skip)],
                dst_ref=out.at[h, mc, pl.ds(skip, an - skip)],
                send_sem=s3.at[h, s], recv_sem=r3.at[h, s],
                device_id={"ch": to}, device_id_type=MESH)
            copy.start()
            third.append(copy)
        inverse_rows(h, mc, 0)
        copy = pltpu.make_async_copy(gsd.at[h, pl.ds(mc * an, an)], out.at[h, mc], own3.at[h])
        copy.start()
        third.append(copy)

    pl.semaphore_wait(barrier, n - 1 + nc - 1)
    gates = []
    for s in order:
        to = lax.rem(mc + s, nc)
        copy = pltpu.make_async_remote_copy(
            src_ref=gate.at[pl.ds(to * an, early), :, cut(0)], dst_ref=grc.at[s],
            send_sem=s4.at[s], recv_sem=r4.at[s],
            device_id={"ch": to}, device_id_type=MESH)
        copy.start()
        gates.append(copy)
    forward(0)
    run(first[0])
    for h in range(halves):
        if h + 1 < halves:
            forward(h + 1)
        for copy in first[h]:
            copy.wait_recv()
        mix(h)
        run(second[h])
        if h + 1 < halves:
            run(first[h + 1])
        finish(h)
    stores = []
    for copy in gates:
        copy.wait()
    for s, copy in fourth:
        copy.wait()

        def step(a, carry):
            value = yrc[s, a]
            smooth = dot(inner[:, :2 * KMAX], jnp.concatenate([value, value], 0))
            ystage[s, a] = (smooth * grc[s, a].astype(F32)).astype(BF16)
            return carry

        lax.fori_loop(0, early, step, 0)
        source = lax.rem(mc + nc - s, nc)
        store = pltpu.make_async_copy(ystage.at[s], out.at[0, source, pl.ds(0, early)], own5.at[s])
        store.start()
        stores.append(store)
    for copy in stores + third:
        copy.wait()
    for copies in first + second:
        for copy in copies:
            copy.wait_send()


def mixing_kernel(nc, halves, nb, gathered, weight, mixing, out):
    size = weight.shape[1]
    per = size // LANES
    tiles = [gathered[h, c].reshape(-1, LANES) for c in range(nc) for h in range(halves)]
    sections = [
        dot(jnp.concatenate(tiles[i * per:(i + 1) * per], 1), weight[i]) for i in range(nb)
    ]
    for k in range(nb):
        total = sections[0] * mixing[k * nb:k * nb + 1]
        for i in range(1, nb):
            total += sections[i] * mixing[k * nb + i:k * nb + i + 1]
        out[:, k * size:(k + 1) * size] = total.astype(BF16)


def local(n, nc, tokens, gating, spectral_gain, device_gain, retained, block_weight, mix_weight):
    rows, width = tokens.shape
    halves = width // LANES
    an = A // nc
    jn = A // n
    early = max(1, an * 5 // 8)
    steps = [jnp.asarray(table) for table in tables()]
    any_space = pl.BlockSpec(memory_space=pl.ANY)
    dma = pltpu.SemaphoreType.DMA
    share = (halves, n, jn, KMAX, LANES)
    gathered = pl.pallas_call(
        functools.partial(filter_kernel, n, nc, halves, early),
        out_shape=jax.ShapeDtypeStruct((halves, nc, an, B, LANES), BF16),
        in_specs=[pl.BlockSpec(memory_space=pltpu.HBM)] * 9,
        out_specs=any_space,
        scratch_shapes=[
            pltpu.VMEM((halves, A, B, LANES), BF16),
            pltpu.VMEM((halves, A, B, LANES), BF16),
            pltpu.VMEM((halves, A, KMAX, LANES), F32),
            pltpu.VMEM((A, KMAX, LANES), F32),
            pltpu.VMEM(share, BF16),
            pltpu.VMEM(share, BF16),
            pltpu.VMEM(share, BF16),
            pltpu.VMEM(share, BF16),
            pltpu.VMEM((halves, A, B, LANES), BF16),
            pltpu.VMEM((nc * early, KMAX, LANES), BF16),
            pltpu.VMEM((nc, early, KMAX, LANES), BF16),
            pltpu.VMEM((nc, early, B, LANES), BF16),
            pltpu.VMEM((nc, early, B, LANES), BF16),
            *[pltpu.VMEM(step.shape, BF16) for step in steps],
            pltpu.VMEM((n, width), F32),
            pltpu.SMEM((LANES,), jnp.int32),
            dma((6,)),
            dma((halves,)), dma((halves,)), dma((halves,)),
            dma((halves, n)), dma((halves, n)), dma((halves, n)), dma((halves, n)),
            dma((halves, nc)), dma((halves, nc)), dma((halves,)),
            dma((nc,)), dma((nc,)), dma((nc,)), dma((nc,)), dma((nc,)),
        ],
        compiler_params=pltpu.CompilerParams(
            collective_id=0, has_side_effects=True, vmem_limit_bytes=60 * 1024 * 1024),
        name="filter",
    )(tokens.reshape(A, B, width), gating.reshape(A, B, width), spectral_gain, device_gain,
      jnp.pad(retained, (0, LANES - retained.shape[0])), *steps)
    nb, size, _ = block_weight.shape
    mixing = jnp.transpose(mix_weight, (1, 2, 0)).reshape(nb * nb, size)
    step = 2 if an % 2 == 0 else 1
    return pl.pallas_call(
        functools.partial(mixing_kernel, nc, halves, nb),
        out_shape=jax.ShapeDtypeStruct((an * B, nb * size), BF16),
        grid=(an // step,),
        in_specs=[
            pl.BlockSpec((halves, nc, step, B, LANES), lambda i: (0, 0, i, 0, 0)),
            pl.BlockSpec(block_weight.shape, lambda i: (0, 0, 0)),
            pl.BlockSpec(mixing.shape, lambda i: (0, 0)),
        ],
        out_specs=pl.BlockSpec((step * B, nb * size), lambda i: (i, 0)),
        compiler_params=pltpu.CompilerParams(vmem_limit_bytes=60 * 1024 * 1024),
        name="mixing",
    )(gathered, block_weight, mixing)


def solution(mesh):
    in_specs = (
        P("seq", "ch"),
        P("seq", "ch"),
        P(None, None, "ch"),
        P(None, "ch"),
        P("ch"),
        P(),
        P(),
    )
    out_specs = P(("seq", "ch"), None)
    body = functools.partial(local, mesh.shape["seq"], mesh.shape["ch"])
    return jax.shard_map(body, mesh=mesh, in_specs=in_specs, out_specs=out_specs, check_vma=False)
```

```python
import functools
import math

import jax
import jax.numpy as jnp
import ml_dtypes
import numpy as np
from jax import lax
from jax.experimental import pallas as pl
from jax.experimental.pallas import tpu as pltpu
from jax.sharding import PartitionSpec as P

GSZ = 16
B = 256
A = 32
KMAX = 128
LANES = 128
MESH = pl.DeviceIdType.MESH
F32 = jnp.float32
BF16 = jnp.bfloat16


def cosine_table(length):
    rows = np.arange(length, dtype=np.float64)[:, None]
    cols = np.arange(length, dtype=np.float64)[None, :]
    table = np.cos(math.pi * (2.0 * cols + 1.0) * rows / (2.0 * length)) * math.sqrt(2.0 / length)
    return np.where(rows == 0.0, table * math.sqrt(0.5), table)


def split(table):
    high = table.astype(ml_dtypes.bfloat16)
    low = (table - high.astype(np.float64)).astype(ml_dtypes.bfloat16)
    return high, low


def tables():
    band_high, band_low = split(cosine_table(B)[:KMAX])
    mid_high, mid_low = split(np.kron(cosine_table(A), np.eye(8)))
    back_high, back_low = split(np.kron(cosine_table(A).T, np.eye(8)))
    return (
        np.concatenate([band_high, band_low], 0),
        np.concatenate([mid_high, mid_low, mid_high], 1),
        np.concatenate([back_high, back_low], 1),
        np.concatenate([band_high.T, band_low.T, band_high.T], 1),
    )


def dot(left, right):
    return jnp.dot(left, right, preferred_element_type=F32)


def two_parts(value):
    high = value.astype(BF16)
    return high, (value - high.astype(F32)).astype(BF16)


def butterfly(parts, levels):
    for level in range(levels):
        angle = 0.6 + 0.1 * level
        cos, sin = math.cos(angle), math.sin(angle)
        mixed = list(parts)
        for low in range(len(parts)):
            if (low >> level) % 2 == 0:
                high = low + (1 << level)
                mixed[low] = cos * parts[low] + sin * parts[high]
                mixed[high] = sin * parts[low] - cos * parts[high]
        parts = mixed
    return parts


def filter_kernel(n, nc, halves, early, tok, gate, gain, dgain, kept,
                  band_hbm, mid_hbm, back_hbm, inner_hbm, out,
                  xt, gt, gn, z, snd, rcv, mxo, bck, gsd, ysd, yrc, grc, ystage,
                  band, mid, back, inner, dg, retained, tsem,
                  xsem, gsem, nsem, s1, r1, s2, r2, s3, r3, own3, s4, r4, s5, r5, own5):
    me = lax.axis_index("seq")
    mc = lax.axis_index("ch")
    levels = n.bit_length() - 1
    jn = A // n
    an = A // nc

    def cut(h):
        return pl.ds(h * LANES, LANES)

    loads = {}
    for h in range(halves):
        loads["x", h] = pltpu.make_async_copy(tok.at[:, :, cut(h)], xt.at[h], xsem.at[h])
        loads["n", h] = pltpu.make_async_copy(gain.at[:, :, cut(h)], gn.at[h], nsem.at[h])
        loads["g", h] = pltpu.make_async_copy(gate.at[:, :, cut(h)], gt.at[h], gsem.at[h])
    for i, (src, dst) in enumerate((
            (band_hbm, band), (mid_hbm, mid), (dgain, dg), (back_hbm, back), (inner_hbm, inner),
            (kept, retained))):
        loads["t", i] = pltpu.make_async_copy(src, dst, tsem.at[i])
    loads["t", 5].start()
    loads["t", 0].start()
    loads["x", 0].start()
    loads["t", 1].start()
    loads["n", 0].start()
    for i in (2, 3, 4):
        loads["t", i].start()
    for h in range(1, halves):
        loads["x", h].start()
        loads["n", h].start()
    for h in range(halves):
        loads["g", h].start()

    barrier = pltpu.get_barrier_semaphore()
    for s in range(1, n):
        pl.semaphore_signal(barrier, inc=1, device_id={"seq": lax.rem(me + s, n)}, device_id_type=MESH)
    for s in range(1, nc):
        pl.semaphore_signal(barrier, inc=1, device_id={"ch": lax.rem(mc + s, nc)}, device_id_type=MESH)

    def forward(h):
        loads["x", h].wait()
        if h == 0:
            loads["t", 0].wait()

        def first(i, carry):
            a = i * 2
            both = dot(band[...], jnp.concatenate([xt[h, a], xt[h, a + 1]], 1))
            both = both[:KMAX] + both[KMAX:]
            z[a] = both[:, :LANES]
            z[a + 1] = both[:, LANES:]
            return carry

        lax.fori_loop(0, A // 2, first, 0, unroll=4)
        loads["n", h].wait()
        if h == 0:
            loads["t", 1].wait()
            loads["t", 5].wait()
        group = lax.broadcasted_iota(jnp.int32, (1, 1, LANES), 2) // GSZ
        keeps = jnp.zeros((1, 1, LANES), jnp.int32)
        for i in range(LANES // GSZ):
            keeps = jnp.where(group == i, retained[h * (LANES // GSZ) + i], keeps)

        def second(kb, carry):
            start = pl.multiple_of(kb * 16, 16)
            block = z[:, pl.ds(start, 16), :]
            pieces = []
            for part in range(2):
                value = block[:, part * 8:part * 8 + 8].reshape(A * 8, LANES)
                high, low = two_parts(value)
                pieces.append(jnp.concatenate([high, high, low], 0))
            value = dot(mid[...], jnp.concatenate(pieces, 1))
            pieces = [value[:, i * LANES:(i + 1) * LANES].reshape(A, 8, LANES) for i in range(2)]
            value = jnp.concatenate(pieces, 1)
            index = start + lax.broadcasted_iota(jnp.int32, (1, 16, LANES), 1)
            value = value * jnp.where(index < keeps, gn[h, :, pl.ds(start, 16), :], 0.0)
            snd[h, :, :, pl.ds(start, 16), :] = value.astype(BF16).reshape(n, jn, 16, LANES)
            return carry

        lax.fori_loop(0, KMAX // 16, second, 0)

    def exchange(src, dst, ssem, rsem, h):
        copies = []
        for s in range(1, n):
            to = lax.rem(me + s, n)
            copies.append(pltpu.make_async_remote_copy(
                src_ref=src.at[h, to], dst_ref=dst.at[h, me],
                send_sem=ssem.at[h, s], recv_sem=rsem.at[h, s],
                device_id={"seq": to}, device_id_type=MESH))
        return copies

    def mix(h):
        rcv[h, me] = snd[h, me]
        if h == 0:
            for i in (2, 3, 4):
                loads["t", i].wait()
        rows = [dg[r:r + 1, h * LANES:(h + 1) * LANES] for r in range(n)]

        def step(i, carry):
            j = i // (KMAX // 16)
            start = pl.multiple_of(lax.rem(i, KMAX // 16) * 16, 16)
            parts = [rcv[h, p, j, pl.ds(start, 16), :].astype(F32) for p in range(n)]
            parts = butterfly(parts, levels)
            parts = [part * row for part, row in zip(parts, rows)]
            parts = butterfly(parts, levels)
            for q in range(n):
                mxo[h, q, j, pl.ds(start, 16), :] = parts[q].astype(BF16)
            return carry

        lax.fori_loop(0, jn * (KMAX // 16), step, 0)
        bck[h, me] = mxo[h, me]

    def inverse_mid(h):
        def step(kb, carry):
            start = pl.multiple_of(kb * 16, 16)
            block = bck[h, :, :, pl.ds(start, 16), :].reshape(A, 16, LANES).astype(F32)
            pieces = [block[:, i * 8:i * 8 + 8].reshape(A * 8, LANES).astype(BF16) for i in range(2)]
            value = jnp.concatenate(pieces, 1)
            value = dot(back[...], jnp.concatenate([value, value], 0))
            for i in range(2):
                part = value[:, i * LANES:(i + 1) * LANES]
                z[:, pl.ds(start + i * 8, 8), :] = part.reshape(A, 8, LANES)
            return carry

        lax.fori_loop(0, KMAX // 16, step, 0)

    def inverse_rows(h, to, skip):
        def step(i, carry):
            a = to * an + skip + i * 2
            high, low = two_parts(jnp.concatenate([z[a], z[a + 1]], 1))
            smooth = dot(inner[...], jnp.concatenate([high, high, low], 0))
            gsd[h, a] = (smooth[:, :LANES] * gt[h, a].astype(F32)).astype(BF16)
            gsd[h, a + 1] = (smooth[:, LANES:] * gt[h, a + 1].astype(F32)).astype(BF16)
            return carry

        lax.fori_loop(0, (an - skip) // 2, step, 0)

    def run(copies):
        for copy in copies:
            copy.start()

    first = [exchange(snd, rcv, s1, r1, h) for h in range(halves)]
    second = [exchange(mxo, bck, s2, r2, h) for h in range(halves)]
    third = []
    fourth = []
    order = [s for level in reversed(range(nc.bit_length() - 1)) for s in range(1 << level, 2 << level)]

    def partner(s):
        to = mc
        for level in range(nc.bit_length() - 1):
            if (s >> level) % 2:
                to = to + (1 << level) - lax.rem(mc // (1 << level), 2) * (2 << level)
        return to


    def finish(h):
        for copy in second[h]:
            copy.wait_recv()
        inverse_mid(h)
        loads["g", h].wait()
        skip = early if h == 0 else 0
        if h == 0:
            for s in order:
                to = partner(s)
                ysd[pl.ds(to * early, early)] = z[pl.ds(to * an, early)].astype(BF16)
                copy = pltpu.make_async_remote_copy(
                    src_ref=ysd.at[pl.ds(to * early, early)], dst_ref=yrc.at[s],
                    send_sem=s5.at[s], recv_sem=r5.at[s],
                    device_id={"ch": to}, device_id_type=MESH)
                copy.start()
                fourth.append((s, copy))
        for s in order:
            to = partner(s)
            inverse_rows(h, to, skip)
            copy = pltpu.make_async_remote_copy(
                src_ref=gsd.at[h, pl.ds(to * an + skip, an - skip)],
                dst_ref=out.at[h, mc, pl.ds(skip, an - skip)],
                send_sem=s3.at[h, s], recv_sem=r3.at[h, s],
                device_id={"ch": to}, device_id_type=MESH)
            copy.start()
            third.append(copy)
        inverse_rows(h, mc, 0)
        copy = pltpu.make_async_copy(gsd.at[h, pl.ds(mc * an, an)], out.at[h, mc], own3.at[h])
        copy.start()
        third.append(copy)

    pl.semaphore_wait(barrier, n - 1 + nc - 1)
    gates = []
    for s in order:
        to = partner(s)
        copy = pltpu.make_async_remote_copy(
            src_ref=gate.at[pl.ds(to * an, early), :, cut(0)], dst_ref=grc.at[s],
            send_sem=s4.at[s], recv_sem=r4.at[s],
            device_id={"ch": to}, device_id_type=MESH)
        copy.start()
        gates.append(copy)
    forward(0)
    run(first[0])
    for h in range(halves):
        if h + 1 < halves:
            forward(h + 1)
        for copy in first[h]:
            copy.wait_recv()
        mix(h)
        run(second[h])
        if h + 1 < halves:
            run(first[h + 1])
        finish(h)
    stores = []
    for copy in gates:
        copy.wait()
    for s, copy in fourth:
        copy.wait()

        def step(i, carry):
            a = i * 2
            value = jnp.concatenate([yrc[s, a], yrc[s, a + 1]], 1)
            smooth = dot(inner[:, :2 * KMAX], jnp.concatenate([value, value], 0))
            ystage[s, a] = (smooth[:, :LANES] * grc[s, a].astype(F32)).astype(BF16)
            ystage[s, a + 1] = (smooth[:, LANES:] * grc[s, a + 1].astype(F32)).astype(BF16)
            return carry

        lax.fori_loop(0, early // 2, step, 0)
        source = partner(s)
        store = pltpu.make_async_copy(ystage.at[s], out.at[0, source, pl.ds(0, early)], own5.at[s])
        store.start()
        stores.append(store)
    for copy in stores + third:
        copy.wait()
    for copies in first + second:
        for copy in copies:
            copy.wait_send()


def mixing_kernel(nc, halves, nb, gathered, weight, mixing, out):
    size = weight.shape[1]
    per = size // LANES
    tiles = [gathered[h, c].reshape(-1, LANES) for c in range(nc) for h in range(halves)]
    sections = [
        dot(jnp.concatenate(tiles[i * per:(i + 1) * per], 1), weight[i]) for i in range(nb)
    ]
    for k in range(nb):
        total = sections[0] * mixing[k, 0:1]
        for i in range(1, nb):
            total += sections[i] * mixing[k, i:i + 1]
        out[:, k * size:(k + 1) * size] = total.astype(BF16)


def local(n, nc, tokens, gating, spectral_gain, device_gain, retained, block_weight, mix_weight):
    rows, width = tokens.shape
    halves = width // LANES
    an = A // nc
    jn = A // n
    early = max(2, an * 3 // 8 * 2)
    steps = [jnp.asarray(table) for table in tables()]
    any_space = pl.BlockSpec(memory_space=pl.ANY)
    dma = pltpu.SemaphoreType.DMA
    share = (halves, n, jn, KMAX, LANES)
    gathered = pl.pallas_call(
        functools.partial(filter_kernel, n, nc, halves, early),
        out_shape=jax.ShapeDtypeStruct((halves, nc, an, B, LANES), BF16),
        in_specs=[pl.BlockSpec(memory_space=pltpu.HBM)] * 9,
        out_specs=any_space,
        scratch_shapes=[
            pltpu.VMEM((halves, A, B, LANES), BF16),
            pltpu.VMEM((halves, A, B, LANES), BF16),
            pltpu.VMEM((halves, A, KMAX, LANES), F32),
            pltpu.VMEM((A, KMAX, LANES), F32),
            pltpu.VMEM(share, BF16),
            pltpu.VMEM(share, BF16),
            pltpu.VMEM(share, BF16),
            pltpu.VMEM(share, BF16),
            pltpu.VMEM((halves, A, B, LANES), BF16),
            pltpu.VMEM((nc * early, KMAX, LANES), BF16),
            pltpu.VMEM((nc, early, KMAX, LANES), BF16),
            pltpu.VMEM((nc, early, B, LANES), BF16),
            pltpu.VMEM((nc, early, B, LANES), BF16),
            *[pltpu.VMEM(step.shape, BF16) for step in steps],
            pltpu.VMEM((n, width), F32),
            pltpu.SMEM(retained.shape, jnp.int32),
            dma((6,)),
            dma((halves,)), dma((halves,)), dma((halves,)),
            dma((halves, n)), dma((halves, n)), dma((halves, n)), dma((halves, n)),
            dma((halves, nc)), dma((halves, nc)), dma((halves,)),
            dma((nc,)), dma((nc,)), dma((nc,)), dma((nc,)), dma((nc,)),
        ],
        compiler_params=pltpu.CompilerParams(
            collective_id=0, has_side_effects=True, vmem_limit_bytes=60 * 1024 * 1024),
        name="filter",
    )(tokens.reshape(A, B, width), gating.reshape(A, B, width), spectral_gain, device_gain,
      retained, *steps)
    nb, size, _ = block_weight.shape
    mixing = jnp.transpose(mix_weight, (1, 2, 0))
    step = 1
    return pl.pallas_call(
        functools.partial(mixing_kernel, nc, halves, nb),
        out_shape=jax.ShapeDtypeStruct((an * B, nb * size), BF16),
        grid=(an // step,),
        in_specs=[
            pl.BlockSpec((halves, nc, step, B, LANES), lambda i: (0, 0, i, 0, 0)),
            pl.BlockSpec(block_weight.shape, lambda i: (0, 0, 0)),
            pl.BlockSpec(mixing.shape, lambda i: (0, 0, 0)),
        ],
        out_specs=pl.BlockSpec((step * B, nb * size), lambda i: (i, 0)),
        compiler_params=pltpu.CompilerParams(vmem_limit_bytes=60 * 1024 * 1024),
        name="mixing",
    )(gathered, block_weight, mixing)


def solution(mesh):
    in_specs = (
        P("seq", "ch"),
        P("seq", "ch"),
        P(None, None, "ch"),
        P(None, "ch"),
        P("ch"),
        P(),
        P(),
    )
    out_specs = P(("seq", "ch"), None)
    body = functools.partial(local, mesh.shape["seq"], mesh.shape["ch"])
    return jax.shard_map(body, mesh=mesh, in_specs=in_specs, out_specs=out_specs, check_vma=False)
```

```python
import functools
import math

import jax
import jax.numpy as jnp
import ml_dtypes
import numpy as np
from jax import lax
from jax.experimental import pallas as pl
from jax.experimental.pallas import tpu as pltpu
from jax.sharding import PartitionSpec as P

GSZ = 16
B = 256
A = 32
KMAX = 128
LANES = 128
MESH = pl.DeviceIdType.MESH
F32 = jnp.float32
BF16 = jnp.bfloat16


def cosine_table(length):
    rows = np.arange(length, dtype=np.float64)[:, None]
    cols = np.arange(length, dtype=np.float64)[None, :]
    table = np.cos(math.pi * (2.0 * cols + 1.0) * rows / (2.0 * length)) * math.sqrt(2.0 / length)
    return np.where(rows == 0.0, table * math.sqrt(0.5), table)


def split(table):
    high = table.astype(ml_dtypes.bfloat16)
    low = (table - high.astype(np.float64)).astype(ml_dtypes.bfloat16)
    return high, low


def tables():
    band_high, band_low = split(cosine_table(B)[:KMAX])
    mid_high, mid_low = split(np.kron(cosine_table(A), np.eye(8)))
    back_high, back_low = split(np.kron(cosine_table(A).T, np.eye(8)))
    return (
        np.concatenate([band_high, band_low], 0),
        np.concatenate([mid_high, mid_low, mid_high], 1),
        np.concatenate([back_high, back_low], 1),
        np.concatenate([band_high.T, band_low.T, band_high.T], 1),
    )


def dot(left, right):
    return jnp.dot(left, right, preferred_element_type=F32)


def two_parts(value):
    high = value.astype(BF16)
    return high, (value - high.astype(F32)).astype(BF16)


def butterfly(parts, levels):
    for level in range(levels):
        angle = 0.6 + 0.1 * level
        cos, sin = math.cos(angle), math.sin(angle)
        mixed = list(parts)
        for low in range(len(parts)):
            if (low >> level) % 2 == 0:
                high = low + (1 << level)
                mixed[low] = cos * parts[low] + sin * parts[high]
                mixed[high] = sin * parts[low] - cos * parts[high]
        parts = mixed
    return parts


def filter_kernel(n, nc, halves, early, tok, gate, gain, dgain, kept,
                  band_hbm, mid_hbm, back_hbm, inner_hbm, out,
                  xt, gt, gn, z, snd, rcv, mxo, bck, gsd, ysd, yrc, grc, ystage,
                  band, mid, back, inner, dg, retained, tsem,
                  xsem, gsem, nsem, s1, r1, s2, r2, s3, r3, own3, s4, r4, s5, r5, own5):
    me = lax.axis_index("seq")
    mc = lax.axis_index("ch")
    levels = n.bit_length() - 1
    jn = A // n
    an = A // nc

    def cut(h):
        return pl.ds(h * LANES, LANES)

    loads = {}
    for h in range(halves):
        loads["x", h] = pltpu.make_async_copy(tok.at[:, :, cut(h)], xt.at[h], xsem.at[h])
        loads["n", h] = pltpu.make_async_copy(gain.at[:, :, cut(h)], gn.at[h], nsem.at[h])
        loads["g", h] = pltpu.make_async_copy(gate.at[:, :, cut(h)], gt.at[h], gsem.at[h])
    for i, (src, dst) in enumerate((
            (band_hbm, band), (mid_hbm, mid), (dgain, dg), (back_hbm, back), (inner_hbm, inner),
            (kept, retained))):
        loads["t", i] = pltpu.make_async_copy(src, dst, tsem.at[i])
    loads["t", 5].start()
    loads["t", 0].start()
    loads["x", 0].start()
    loads["t", 1].start()
    loads["n", 0].start()
    for i in (2, 3, 4):
        loads["t", i].start()
    for h in range(1, halves):
        loads["x", h].start()
        loads["n", h].start()
    for h in range(halves):
        loads["g", h].start()

    barrier = pltpu.get_barrier_semaphore()
    for s in range(1, n):
        pl.semaphore_signal(barrier, inc=1, device_id={"seq": lax.rem(me + s, n)}, device_id_type=MESH)
    for s in range(1, nc):
        pl.semaphore_signal(barrier, inc=1, device_id={"ch": lax.rem(mc + s, nc)}, device_id_type=MESH)

    def forward(h):
        loads["x", h].wait()
        if h == 0:
            loads["t", 0].wait()

        def first(i, carry):
            a = i * 2
            both = dot(band[...], jnp.concatenate([xt[h, a], xt[h, a + 1]], 1))
            both = both[:KMAX] + both[KMAX:]
            z[a] = both[:, :LANES]
            z[a + 1] = both[:, LANES:]
            return carry

        lax.fori_loop(0, A // 2, first, 0, unroll=4)
        loads["n", h].wait()
        if h == 0:
            loads["t", 1].wait()
            loads["t", 5].wait()
        group = lax.broadcasted_iota(jnp.int32, (1, 1, LANES), 2) // GSZ
        keeps = jnp.zeros((1, 1, LANES), jnp.int32)
        for i in range(LANES // GSZ):
            keeps = jnp.where(group == i, retained[h * (LANES // GSZ) + i], keeps)

        def second(kb, carry):
            start = pl.multiple_of(kb * 16, 16)
            block = z[:, pl.ds(start, 16), :]
            pieces = []
            for part in range(2):
                value = block[:, part * 8:part * 8 + 8].reshape(A * 8, LANES)
                high, low = two_parts(value)
                pieces.append(jnp.concatenate([high, high, low], 0))
            value = dot(mid[...], jnp.concatenate(pieces, 1))
            pieces = [value[:, i * LANES:(i + 1) * LANES].reshape(A, 8, LANES) for i in range(2)]
            value = jnp.concatenate(pieces, 1)
            index = start + lax.broadcasted_iota(jnp.int32, (1, 16, LANES), 1)
            value = value * jnp.where(index < keeps, gn[h, :, pl.ds(start, 16), :], 0.0)
            snd[h, :, :, pl.ds(start, 16), :] = value.astype(BF16).reshape(n, jn, 16, LANES)
            return carry

        lax.fori_loop(0, KMAX // 16, second, 0)

    def exchange(src, dst, ssem, rsem, h):
        copies = []
        for s in range(1, n):
            to = lax.rem(me + s, n)
            copies.append(pltpu.make_async_remote_copy(
                src_ref=src.at[h, to], dst_ref=dst.at[h, me],
                send_sem=ssem.at[h, s], recv_sem=rsem.at[h, s],
                device_id={"seq": to}, device_id_type=MESH))
        return copies

    def mix(h):
        rcv[h, me] = snd[h, me]
        if h == 0:
            for i in (2, 3, 4):
                loads["t", i].wait()
        rows = [dg[r:r + 1, h * LANES:(h + 1) * LANES] for r in range(n)]

        def step(i, carry):
            j = i // (KMAX // 16)
            start = pl.multiple_of(lax.rem(i, KMAX // 16) * 16, 16)
            parts = [rcv[h, p, j, pl.ds(start, 16), :].astype(F32) for p in range(n)]
            parts = butterfly(parts, levels)
            parts = [part * row for part, row in zip(parts, rows)]
            parts = butterfly(parts, levels)
            for q in range(n):
                mxo[h, q, j, pl.ds(start, 16), :] = parts[q].astype(BF16)
            return carry

        lax.fori_loop(0, jn * (KMAX // 16), step, 0)
        bck[h, me] = mxo[h, me]

    def inverse_mid(h):
        def step(kb, carry):
            start = pl.multiple_of(kb * 16, 16)
            block = bck[h, :, :, pl.ds(start, 16), :].reshape(A, 16, LANES).astype(F32)
            pieces = [block[:, i * 8:i * 8 + 8].reshape(A * 8, LANES).astype(BF16) for i in range(2)]
            value = jnp.concatenate(pieces, 1)
            value = dot(back[...], jnp.concatenate([value, value], 0))
            for i in range(2):
                part = value[:, i * LANES:(i + 1) * LANES]
                z[:, pl.ds(start + i * 8, 8), :] = part.reshape(A, 8, LANES)
            return carry

        lax.fori_loop(0, KMAX // 16, step, 0)

    def inverse_rows(h, to, skip):
        def step(i, carry):
            a = to * an + skip + i * 2
            high, low = two_parts(jnp.concatenate([z[a], z[a + 1]], 1))
            smooth = dot(inner[...], jnp.concatenate([high, high, low], 0))
            gsd[h, a] = (smooth[:, :LANES] * gt[h, a].astype(F32)).astype(BF16)
            gsd[h, a + 1] = (smooth[:, LANES:] * gt[h, a + 1].astype(F32)).astype(BF16)
            return carry

        lax.fori_loop(0, (an - skip) // 2, step, 0)

    def run(copies):
        for copy in copies:
            copy.start()

    first = [exchange(snd, rcv, s1, r1, h) for h in range(halves)]
    second = [exchange(mxo, bck, s2, r2, h) for h in range(halves)]
    third = []
    fourth = []
    crossing = [s for level in reversed(range(nc.bit_length() - 1)) for s in range(1 << level, 2 << level)]

    outer = 1 - lax.rem((mc + nc // 4) // (nc // 2), 2)
    order = [s + outer * (i + 1 - s) for i, s in enumerate(crossing)]

    def partner(s):
        to = mc
        for level in range(nc.bit_length() - 1):
            flip = lax.rem(s // (1 << level), 2)
            to = to + flip * ((1 << level) - lax.rem(mc // (1 << level), 2) * (2 << level))
        return to


    def finish(h):
        for copy in second[h]:
            copy.wait_recv()
        inverse_mid(h)
        loads["g", h].wait()
        skip = early if h == 0 else 0
        if h == 0:
            for s in order:
                to = partner(s)
                ysd[pl.ds(to * early, early)] = z[pl.ds(to * an, early)].astype(BF16)
                copy = pltpu.make_async_remote_copy(
                    src_ref=ysd.at[pl.ds(to * early, early)], dst_ref=yrc.at[s],
                    send_sem=s5.at[s], recv_sem=r5.at[s],
                    device_id={"ch": to}, device_id_type=MESH)
                copy.start()
                fourth.append((s, copy))
        for s in order:
            to = partner(s)
            inverse_rows(h, to, skip)
            copy = pltpu.make_async_remote_copy(
                src_ref=gsd.at[h, pl.ds(to * an + skip, an - skip)],
                dst_ref=out.at[h, mc, pl.ds(skip, an - skip)],
                send_sem=s3.at[h, s], recv_sem=r3.at[h, s],
                device_id={"ch": to}, device_id_type=MESH)
            copy.start()
            third.append(copy)
        inverse_rows(h, mc, 0)
        copy = pltpu.make_async_copy(gsd.at[h, pl.ds(mc * an, an)], out.at[h, mc], own3.at[h])
        copy.start()
        third.append(copy)

    pl.semaphore_wait(barrier, n - 1 + nc - 1)
    gates = []
    for s in order:
        to = partner(s)
        copy = pltpu.make_async_remote_copy(
            src_ref=gate.at[pl.ds(to * an, early), :, cut(0)], dst_ref=grc.at[s],
            send_sem=s4.at[s], recv_sem=r4.at[s],
            device_id={"ch": to}, device_id_type=MESH)
        copy.start()
        gates.append(copy)
    forward(0)
    run(first[0])
    for h in range(halves):
        if h + 1 < halves:
            forward(h + 1)
        for copy in first[h]:
            copy.wait_recv()
        mix(h)
        run(second[h])
        if h + 1 < halves:
            run(first[h + 1])
        finish(h)
    stores = []
    for copy in gates:
        copy.wait()
    for s, copy in fourth:
        copy.wait()

        def step(i, carry):
            a = i * 2
            value = jnp.concatenate([yrc[s, a], yrc[s, a + 1]], 1)
            smooth = dot(inner[:, :2 * KMAX], jnp.concatenate([value, value], 0))
            ystage[s, a] = (smooth[:, :LANES] * grc[s, a].astype(F32)).astype(BF16)
            ystage[s, a + 1] = (smooth[:, LANES:] * grc[s, a + 1].astype(F32)).astype(BF16)
            return carry

        lax.fori_loop(0, early // 2, step, 0)
        source = partner(s)
        store = pltpu.make_async_copy(ystage.at[s], out.at[0, source, pl.ds(0, early)], own5.at[s])
        store.start()
        stores.append(store)
    for copy in stores + third:
        copy.wait()
    for copies in first + second:
        for copy in copies:
            copy.wait_send()


def mixing_kernel(nc, halves, nb, gathered, weight, mixing, out):
    size = weight.shape[1]
    per = size // LANES
    tiles = [gathered[h, c].reshape(-1, LANES) for c in range(nc) for h in range(halves)]
    sections = [
        dot(jnp.concatenate(tiles[i * per:(i + 1) * per], 1), weight[i]) for i in range(nb)
    ]
    for k in range(nb):
        total = sections[0] * mixing[k, 0:1]
        for i in range(1, nb):
            total += sections[i] * mixing[k, i:i + 1]
        out[:, k * size:(k + 1) * size] = total.astype(BF16)


def local(n, nc, tokens, gating, spectral_gain, device_gain, retained, block_weight, mix_weight):
    rows, width = tokens.shape
    halves = width // LANES
    an = A // nc
    jn = A // n
    early = max(2, an * 3 // 8 * 2)
    steps = [jnp.asarray(table) for table in tables()]
    any_space = pl.BlockSpec(memory_space=pl.ANY)
    dma = pltpu.SemaphoreType.DMA
    share = (halves, n, jn, KMAX, LANES)
    gathered = pl.pallas_call(
        functools.partial(filter_kernel, n, nc, halves, early),
        out_shape=jax.ShapeDtypeStruct((halves, nc, an, B, LANES), BF16),
        in_specs=[pl.BlockSpec(memory_space=pltpu.HBM)] * 9,
        out_specs=any_space,
        scratch_shapes=[
            pltpu.VMEM((halves, A, B, LANES), BF16),
            pltpu.VMEM((halves, A, B, LANES), BF16),
            pltpu.VMEM((halves, A, KMAX, LANES), F32),
            pltpu.VMEM((A, KMAX, LANES), F32),
            pltpu.VMEM(share, BF16),
            pltpu.VMEM(share, BF16),
            pltpu.VMEM(share, BF16),
            pltpu.VMEM(share, BF16),
            pltpu.VMEM((halves, A, B, LANES), BF16),
            pltpu.VMEM((nc * early, KMAX, LANES), BF16),
            pltpu.VMEM((nc, early, KMAX, LANES), BF16),
            pltpu.VMEM((nc, early, B, LANES), BF16),
            pltpu.VMEM((nc, early, B, LANES), BF16),
            *[pltpu.VMEM(step.shape, BF16) for step in steps],
            pltpu.VMEM((n, width), F32),
            pltpu.SMEM(retained.shape, jnp.int32),
            dma((6,)),
            dma((halves,)), dma((halves,)), dma((halves,)),
            dma((halves, n)), dma((halves, n)), dma((halves, n)), dma((halves, n)),
            dma((halves, nc)), dma((halves, nc)), dma((halves,)),
            dma((nc,)), dma((nc,)), dma((nc,)), dma((nc,)), dma((nc,)),
        ],
        compiler_params=pltpu.CompilerParams(
            collective_id=0, has_side_effects=True, vmem_limit_bytes=60 * 1024 * 1024),
        name="filter",
    )(tokens.reshape(A, B, width), gating.reshape(A, B, width), spectral_gain, device_gain,
      retained, *steps)
    nb, size, _ = block_weight.shape
    mixing = jnp.transpose(mix_weight, (1, 2, 0))
    step = 2 if an % 2 == 0 else 1
    return pl.pallas_call(
        functools.partial(mixing_kernel, nc, halves, nb),
        out_shape=jax.ShapeDtypeStruct((an * B, nb * size), BF16),
        grid=(an // step,),
        in_specs=[
            pl.BlockSpec((halves, nc, step, B, LANES), lambda i: (0, 0, i, 0, 0)),
            pl.BlockSpec(block_weight.shape, lambda i: (0, 0, 0)),
            pl.BlockSpec(mixing.shape, lambda i: (0, 0, 0)),
        ],
        out_specs=pl.BlockSpec((step * B, nb * size), lambda i: (i, 0)),
        compiler_params=pltpu.CompilerParams(vmem_limit_bytes=60 * 1024 * 1024),
        name="mixing",
    )(gathered, block_weight, mixing)


def solution(mesh):
    in_specs = (
        P("seq", "ch"),
        P("seq", "ch"),
        P(None, None, "ch"),
        P(None, "ch"),
        P("ch"),
        P(),
        P(),
    )
    out_specs = P(("seq", "ch"), None)
    body = functools.partial(local, mesh.shape["seq"], mesh.shape["ch"])
    return jax.shard_map(body, mesh=mesh, in_specs=in_specs, out_specs=out_specs, check_vma=False)
```

```python
import functools
import math

import jax
import jax.numpy as jnp
import ml_dtypes
import numpy as np
from jax import lax
from jax.experimental import pallas as pl
from jax.experimental.pallas import tpu as pltpu
from jax.sharding import PartitionSpec as P

GSZ = 16
B = 256
A = 32
KMAX = 128
LANES = 128
MESH = pl.DeviceIdType.MESH
F32 = jnp.float32
BF16 = jnp.bfloat16


def cosine_table(length):
    rows = np.arange(length, dtype=np.float64)[:, None]
    cols = np.arange(length, dtype=np.float64)[None, :]
    table = np.cos(math.pi * (2.0 * cols + 1.0) * rows / (2.0 * length)) * math.sqrt(2.0 / length)
    return np.where(rows == 0.0, table * math.sqrt(0.5), table)


def split(table):
    high = table.astype(ml_dtypes.bfloat16)
    low = (table - high.astype(np.float64)).astype(ml_dtypes.bfloat16)
    return high, low


def tables():
    band_high, band_low = split(cosine_table(B)[:KMAX])
    mid_high, mid_low = split(np.kron(cosine_table(A), np.eye(8)))
    back_high, back_low = split(np.kron(cosine_table(A).T, np.eye(8)))
    return (
        np.concatenate([band_high, band_low], 0),
        np.concatenate([mid_high, mid_low, mid_high], 1),
        np.concatenate([back_high, back_low], 1),
        np.concatenate([band_high.T, band_low.T, band_high.T], 1),
    )


def dot(left, right):
    return jnp.dot(left, right, preferred_element_type=F32)


def two_parts(value):
    high = value.astype(BF16)
    return high, (value - high.astype(F32)).astype(BF16)


def butterfly(parts, levels):
    for level in range(levels):
        angle = 0.6 + 0.1 * level
        cos, sin = math.cos(angle), math.sin(angle)
        mixed = list(parts)
        for low in range(len(parts)):
            if (low >> level) % 2 == 0:
                high = low + (1 << level)
                mixed[low] = cos * parts[low] + sin * parts[high]
                mixed[high] = sin * parts[low] - cos * parts[high]
        parts = mixed
    return parts


def filter_kernel(n, nc, halves, early, tok, gate, gain, dgain, kept,
                  band_hbm, mid_hbm, back_hbm, inner_hbm, out,
                  xt, gt, gn, z, snd, rcv, mxo, bck, gsd, ysd, yrc, grc, ystage,
                  band, mid, back, inner, dg, retained, tsem,
                  xsem, gsem, nsem, s1, r1, s2, r2, s3, r3, own3, s4, r4, s5, r5, own5):
    me = lax.axis_index("seq")
    mc = lax.axis_index("ch")
    levels = n.bit_length() - 1
    jn = A // n
    an = A // nc

    def cut(h):
        return pl.ds(h * LANES, LANES)

    loads = {}
    for h in range(halves):
        loads["x", h] = pltpu.make_async_copy(tok.at[:, :, cut(h)], xt.at[h], xsem.at[h])
        loads["n", h] = pltpu.make_async_copy(gain.at[:, :, cut(h)], gn.at[h], nsem.at[h])
        loads["g", h] = pltpu.make_async_copy(gate.at[:, :, cut(h)], gt.at[h], gsem.at[h])
    for i, (src, dst) in enumerate((
            (band_hbm, band), (mid_hbm, mid), (dgain, dg), (back_hbm, back), (inner_hbm, inner),
            (kept, retained))):
        loads["t", i] = pltpu.make_async_copy(src, dst, tsem.at[i])
    loads["t", 5].start()
    loads["t", 0].start()
    loads["x", 0].start()
    loads["t", 1].start()
    loads["n", 0].start()
    for i in (2, 3, 4):
        loads["t", i].start()
    for h in range(1, halves):
        loads["x", h].start()
        loads["n", h].start()
    for h in range(halves):
        loads["g", h].start()

    barrier = pltpu.get_barrier_semaphore()
    for s in range(1, n):
        pl.semaphore_signal(barrier, inc=1, device_id={"seq": lax.rem(me + s, n)}, device_id_type=MESH)
    for s in range(1, nc):
        pl.semaphore_signal(barrier, inc=1, device_id={"ch": lax.rem(mc + s, nc)}, device_id_type=MESH)

    def forward(h):
        loads["x", h].wait()
        if h == 0:
            loads["t", 0].wait()

        def first(i, carry):
            a = i * 2
            both = dot(band[...], jnp.concatenate([xt[h, a], xt[h, a + 1]], 1))
            both = both[:KMAX] + both[KMAX:]
            z[a] = both[:, :LANES]
            z[a + 1] = both[:, LANES:]
            return carry

        lax.fori_loop(0, A // 2, first, 0, unroll=4)
        loads["n", h].wait()
        if h == 0:
            loads["t", 1].wait()
            loads["t", 5].wait()
        group = lax.broadcasted_iota(jnp.int32, (1, 1, LANES), 2) // GSZ
        keeps = jnp.zeros((1, 1, LANES), jnp.int32)
        for i in range(LANES // GSZ):
            keeps = jnp.where(group == i, retained[h * (LANES // GSZ) + i], keeps)

        def second(kb, carry):
            start = pl.multiple_of(kb * 16, 16)
            block = z[:, pl.ds(start, 16), :]
            pieces = []
            for part in range(2):
                value = block[:, part * 8:part * 8 + 8].reshape(A * 8, LANES)
                high, low = two_parts(value)
                pieces.append(jnp.concatenate([high, high, low], 0))
            value = dot(mid[...], jnp.concatenate(pieces, 1))
            pieces = [value[:, i * LANES:(i + 1) * LANES].reshape(A, 8, LANES) for i in range(2)]
            value = jnp.concatenate(pieces, 1)
            index = start + lax.broadcasted_iota(jnp.int32, (1, 16, LANES), 1)
            value = value * jnp.where(index < keeps, gn[h, :, pl.ds(start, 16), :], 0.0)
            snd[h, :, :, pl.ds(start, 16), :] = value.astype(BF16).reshape(n, jn, 16, LANES)
            return carry

        lax.fori_loop(0, KMAX // 16, second, 0)

    def exchange(src, dst, ssem, rsem, h):
        copies = []
        for s in range(1, n):
            to = lax.rem(me + s, n)
            copies.append(pltpu.make_async_remote_copy(
                src_ref=src.at[h, to], dst_ref=dst.at[h, me],
                send_sem=ssem.at[h, s], recv_sem=rsem.at[h, s],
                device_id={"seq": to}, device_id_type=MESH))
        return copies

    def mix(h):
        rcv[h, me] = snd[h, me]
        if h == 0:
            for i in (2, 3, 4):
                loads["t", i].wait()
        rows = [dg[r:r + 1, h * LANES:(h + 1) * LANES] for r in range(n)]

        def step(i, carry):
            j = i // (KMAX // 16)
            start = pl.multiple_of(lax.rem(i, KMAX // 16) * 16, 16)
            parts = [rcv[h, p, j, pl.ds(start, 16), :].astype(F32) for p in range(n)]
            parts = butterfly(parts, levels)
            parts = [part * row for part, row in zip(parts, rows)]
            parts = butterfly(parts, levels)
            for q in range(n):
                mxo[h, q, j, pl.ds(start, 16), :] = parts[q].astype(BF16)
            return carry

        lax.fori_loop(0, jn * (KMAX // 16), step, 0)
        bck[h, me] = mxo[h, me]

    def inverse_mid(h):
        def step(kb, carry):
            start = pl.multiple_of(kb * 16, 16)
            block = bck[h, :, :, pl.ds(start, 16), :].reshape(A, 16, LANES).astype(F32)
            pieces = [block[:, i * 8:i * 8 + 8].reshape(A * 8, LANES).astype(BF16) for i in range(2)]
            value = jnp.concatenate(pieces, 1)
            value = dot(back[...], jnp.concatenate([value, value], 0))
            for i in range(2):
                part = value[:, i * LANES:(i + 1) * LANES]
                z[:, pl.ds(start + i * 8, 8), :] = part.reshape(A, 8, LANES)
            return carry

        lax.fori_loop(0, KMAX // 16, step, 0)

    def inverse_rows(h, to, skip):
        def step(i, carry):
            a = to * an + skip + i * 2
            high, low = two_parts(jnp.concatenate([z[a], z[a + 1]], 1))
            smooth = dot(inner[...], jnp.concatenate([high, high, low], 0))
            gsd[h, a] = (smooth[:, :LANES] * gt[h, a].astype(F32)).astype(BF16)
            gsd[h, a + 1] = (smooth[:, LANES:] * gt[h, a + 1].astype(F32)).astype(BF16)
            return carry

        lax.fori_loop(0, (an - skip) // 2, step, 0)
        if (an - skip) % 2:
            a = to * an + an - 1
            high, low = two_parts(z[a])
            smooth = dot(inner[...], jnp.concatenate([high, high, low], 0))
            gsd[h, a] = (smooth * gt[h, a].astype(F32)).astype(BF16)

    def run(copies):
        for copy in copies:
            copy.start()

    first = [exchange(snd, rcv, s1, r1, h) for h in range(halves)]
    second = [exchange(mxo, bck, s2, r2, h) for h in range(halves)]
    third = []
    fourth = []
    crossing = [s for level in reversed(range(nc.bit_length() - 1)) for s in range(1 << level, 2 << level)]

    outer = 1 - lax.rem((mc + nc // 4) // (nc // 2), 2)
    order = [s + outer * (i + 1 - s) for i, s in enumerate(crossing)]

    def partner(s):
        to = mc
        for level in range(nc.bit_length() - 1):
            flip = lax.rem(s // (1 << level), 2)
            to = to + flip * ((1 << level) - lax.rem(mc // (1 << level), 2) * (2 << level))
        return to


    def finish(h):
        for copy in second[h]:
            copy.wait_recv()
        inverse_mid(h)
        loads["g", h].wait()
        skip = early if h == 0 else 0
        if h == 0:
            for s in order:
                to = partner(s)
                ysd[pl.ds(to * early, early)] = z[pl.ds(to * an, early)].astype(BF16)
                copy = pltpu.make_async_remote_copy(
                    src_ref=ysd.at[pl.ds(to * early, early)], dst_ref=yrc.at[s],
                    send_sem=s5.at[s], recv_sem=r5.at[s],
                    device_id={"ch": to}, device_id_type=MESH)
                copy.start()
                fourth.append((s, copy))
        for s in order:
            to = partner(s)
            inverse_rows(h, to, skip)
            copy = pltpu.make_async_remote_copy(
                src_ref=gsd.at[h, pl.ds(to * an + skip, an - skip)],
                dst_ref=out.at[h, mc, pl.ds(skip, an - skip)],
                send_sem=s3.at[h, s], recv_sem=r3.at[h, s],
                device_id={"ch": to}, device_id_type=MESH)
            copy.start()
            third.append(copy)
        inverse_rows(h, mc, 0)
        copy = pltpu.make_async_copy(gsd.at[h, pl.ds(mc * an, an)], out.at[h, mc], own3.at[h])
        copy.start()
        third.append(copy)

    pl.semaphore_wait(barrier, n - 1 + nc - 1)
    gates = []
    for s in order:
        to = partner(s)
        copy = pltpu.make_async_remote_copy(
            src_ref=gate.at[pl.ds(to * an, early), :, cut(0)], dst_ref=grc.at[s],
            send_sem=s4.at[s], recv_sem=r4.at[s],
            device_id={"ch": to}, device_id_type=MESH)
        copy.start()
        gates.append(copy)
    forward(0)
    run(first[0])
    for h in range(halves):
        if h + 1 < halves:
            forward(h + 1)
        for copy in first[h]:
            copy.wait_recv()
        mix(h)
        run(second[h])
        if h + 1 < halves:
            run(first[h + 1])
        finish(h)
    stores = []
    for copy in gates:
        copy.wait()
    for s, copy in fourth:
        copy.wait()

        def step(i, carry):
            a = i * 2
            value = jnp.concatenate([yrc[s, a], yrc[s, a + 1]], 1)
            smooth = dot(inner[:, :2 * KMAX], jnp.concatenate([value, value], 0))
            ystage[s, a] = (smooth[:, :LANES] * grc[s, a].astype(F32)).astype(BF16)
            ystage[s, a + 1] = (smooth[:, LANES:] * grc[s, a + 1].astype(F32)).astype(BF16)
            return carry

        lax.fori_loop(0, early // 2, step, 0)
        if early % 2:
            a = early - 1
            value = yrc[s, a]
            smooth = dot(inner[:, :2 * KMAX], jnp.concatenate([value, value], 0))
            ystage[s, a] = (smooth * grc[s, a].astype(F32)).astype(BF16)
        source = partner(s)
        store = pltpu.make_async_copy(ystage.at[s], out.at[0, source, pl.ds(0, early)], own5.at[s])
        store.start()
        stores.append(store)
    for copy in stores + third:
        copy.wait()
    for copies in first + second:
        for copy in copies:
            copy.wait_send()


def mixing_kernel(nc, halves, nb, gathered, weight, mixing, out):
    size = weight.shape[1]
    per = size // LANES
    tiles = [gathered[h, c].reshape(-1, LANES) for c in range(nc) for h in range(halves)]
    sections = [
        dot(jnp.concatenate(tiles[i * per:(i + 1) * per], 1), weight[i]) for i in range(nb)
    ]
    for k in range(nb):
        total = sections[0] * mixing[k, 0:1]
        for i in range(1, nb):
            total += sections[i] * mixing[k, i:i + 1]
        out[:, k * size:(k + 1) * size] = total.astype(BF16)


def local(n, nc, tokens, gating, spectral_gain, device_gain, retained, block_weight, mix_weight):
    rows, width = tokens.shape
    halves = width // LANES
    an = A // nc
    jn = A // n
    early = max(1, an * 5 // 8)
    steps = [jnp.asarray(table) for table in tables()]
    any_space = pl.BlockSpec(memory_space=pl.ANY)
    dma = pltpu.SemaphoreType.DMA
    share = (halves, n, jn, KMAX, LANES)
    gathered = pl.pallas_call(
        functools.partial(filter_kernel, n, nc, halves, early),
        out_shape=jax.ShapeDtypeStruct((halves, nc, an, B, LANES), BF16),
        in_specs=[pl.BlockSpec(memory_space=pltpu.HBM)] * 9,
        out_specs=any_space,
        scratch_shapes=[
            pltpu.VMEM((halves, A, B, LANES), BF16),
            pltpu.VMEM((halves, A, B, LANES), BF16),
            pltpu.VMEM((halves, A, KMAX, LANES), F32),
            pltpu.VMEM((A, KMAX, LANES), F32),
            pltpu.VMEM(share, BF16),
            pltpu.VMEM(share, BF16),
            pltpu.VMEM(share, BF16),
            pltpu.VMEM(share, BF16),
            pltpu.VMEM((halves, A, B, LANES), BF16),
            pltpu.VMEM((nc * early, KMAX, LANES), BF16),
            pltpu.VMEM((nc, early, KMAX, LANES), BF16),
            pltpu.VMEM((nc, early, B, LANES), BF16),
            pltpu.VMEM((nc, early, B, LANES), BF16),
            *[pltpu.VMEM(step.shape, BF16) for step in steps],
            pltpu.VMEM((n, width), F32),
            pltpu.SMEM(retained.shape, jnp.int32),
            dma((6,)),
            dma((halves,)), dma((halves,)), dma((halves,)),
            dma((halves, n)), dma((halves, n)), dma((halves, n)), dma((halves, n)),
            dma((halves, nc)), dma((halves, nc)), dma((halves,)),
            dma((nc,)), dma((nc,)), dma((nc,)), dma((nc,)), dma((nc,)),
        ],
        compiler_params=pltpu.CompilerParams(
            collective_id=0, has_side_effects=True, vmem_limit_bytes=60 * 1024 * 1024),
        name="filter",
    )(tokens.reshape(A, B, width), gating.reshape(A, B, width), spectral_gain, device_gain,
      retained, *steps)
    nb, size, _ = block_weight.shape
    mixing = jnp.transpose(mix_weight, (1, 2, 0))
    step = 4 if an % 4 == 0 else 1
    return pl.pallas_call(
        functools.partial(mixing_kernel, nc, halves, nb),
        out_shape=jax.ShapeDtypeStruct((an * B, nb * size), BF16),
        grid=(an // step,),
        in_specs=[
            pl.BlockSpec((halves, nc, step, B, LANES), lambda i: (0, 0, i, 0, 0)),
            pl.BlockSpec(block_weight.shape, lambda i: (0, 0, 0)),
            pl.BlockSpec(mixing.shape, lambda i: (0, 0, 0)),
        ],
        out_specs=pl.BlockSpec((step * B, nb * size), lambda i: (i, 0)),
        compiler_params=pltpu.CompilerParams(vmem_limit_bytes=60 * 1024 * 1024),
        name="mixing",
    )(gathered, block_weight, mixing)


def solution(mesh):
    in_specs = (
        P("seq", "ch"),
        P("seq", "ch"),
        P(None, None, "ch"),
        P(None, "ch"),
        P("ch"),
        P(),
        P(),
    )
    out_specs = P(("seq", "ch"), None)
    body = functools.partial(local, mesh.shape["seq"], mesh.shape["ch"])
    return jax.shard_map(body, mesh=mesh, in_specs=in_specs, out_specs=out_specs, check_vma=False)
```

```python
import functools
import math

import jax
import jax.numpy as jnp
import ml_dtypes
import numpy as np
from jax import lax
from jax.experimental import pallas as pl
from jax.experimental.pallas import tpu as pltpu
from jax.sharding import PartitionSpec as P

GSZ = 16
B = 256
A = 32
KMAX = 128
LANES = 128
MESH = pl.DeviceIdType.MESH
F32 = jnp.float32
BF16 = jnp.bfloat16


def cosine_table(length):
    rows = np.arange(length, dtype=np.float64)[:, None]
    cols = np.arange(length, dtype=np.float64)[None, :]
    table = np.cos(math.pi * (2.0 * cols + 1.0) * rows / (2.0 * length)) * math.sqrt(2.0 / length)
    return np.where(rows == 0.0, table * math.sqrt(0.5), table)


def split(table):
    high = table.astype(ml_dtypes.bfloat16)
    low = (table - high.astype(np.float64)).astype(ml_dtypes.bfloat16)
    return high, low


def tables():
    band_high, band_low = split(cosine_table(B)[:KMAX])
    mid_high, mid_low = split(np.kron(cosine_table(A), np.eye(8)))
    back_high, back_low = split(np.kron(cosine_table(A).T, np.eye(8)))
    return (
        np.concatenate([band_high, band_low], 0),
        np.concatenate([mid_high, mid_low, mid_high], 1),
        np.concatenate([back_high, back_low], 1),
        np.concatenate([band_high.T, band_low.T, band_high.T], 1),
    )


def dot(left, right):
    return jnp.dot(left, right, preferred_element_type=F32)


def two_parts(value):
    high = value.astype(BF16)
    return high, (value - high.astype(F32)).astype(BF16)


def butterfly(parts, levels):
    for level in range(levels):
        angle = 0.6 + 0.1 * level
        cos, sin = math.cos(angle), math.sin(angle)
        mixed = list(parts)
        for low in range(len(parts)):
            if (low >> level) % 2 == 0:
                high = low + (1 << level)
                mixed[low] = cos * parts[low] + sin * parts[high]
                mixed[high] = sin * parts[low] - cos * parts[high]
        parts = mixed
    return parts


def filter_kernel(n, nc, halves, early, tok, gate, gain, dgain, kept,
                  band_hbm, mid_hbm, back_hbm, inner_hbm, out,
                  xt, gt, gn, z, snd, rcv, mxo, bck, gsd, ysd, yrc, grc, ystage,
                  band, mid, back, inner, dg, retained, tsem,
                  xsem, gsem, nsem, s1, r1, s2, r2, s3, r3, own3, s4, r4, s5, r5, own5):
    me = lax.axis_index("seq")
    mc = lax.axis_index("ch")
    levels = n.bit_length() - 1
    jn = A // n
    an = A // nc

    def cut(h):
        return pl.ds(h * LANES, LANES)

    loads = {}
    for h in range(halves):
        loads["x", h] = pltpu.make_async_copy(tok.at[:, :, cut(h)], xt.at[h], xsem.at[h])
        loads["n", h] = pltpu.make_async_copy(gain.at[:, :, cut(h)], gn.at[h], nsem.at[h])
        loads["g", h] = pltpu.make_async_copy(gate.at[:, :, cut(h)], gt.at[h], gsem.at[h])
    for i, (src, dst) in enumerate((
            (band_hbm, band), (mid_hbm, mid), (dgain, dg), (back_hbm, back), (inner_hbm, inner),
            (kept, retained))):
        loads["t", i] = pltpu.make_async_copy(src, dst, tsem.at[i])
    loads["t", 5].start()
    loads["t", 0].start()
    loads["x", 0].start()
    loads["t", 1].start()
    loads["n", 0].start()
    for i in (2, 3, 4):
        loads["t", i].start()
    for h in range(1, halves):
        loads["x", h].start()
        loads["n", h].start()
    for h in range(halves):
        loads["g", h].start()

    barrier = pltpu.get_barrier_semaphore()
    for s in range(1, n):
        pl.semaphore_signal(barrier, inc=1, device_id={"seq": lax.rem(me + s, n)}, device_id_type=MESH)
    for s in range(1, nc):
        pl.semaphore_signal(barrier, inc=1, device_id={"ch": lax.rem(mc + s, nc)}, device_id_type=MESH)

    def forward(h):
        loads["x", h].wait()
        if h == 0:
            loads["t", 0].wait()

        def first(i, carry):
            a = i * 2
            both = dot(band[...], jnp.concatenate([xt[h, a], xt[h, a + 1]], 1))
            both = both[:KMAX] + both[KMAX:]
            z[a] = both[:, :LANES]
            z[a + 1] = both[:, LANES:]
            return carry

        lax.fori_loop(0, A // 2, first, 0, unroll=4)
        loads["n", h].wait()
        if h == 0:
            loads["t", 1].wait()
            loads["t", 5].wait()
        group = lax.broadcasted_iota(jnp.int32, (1, 1, LANES), 2) // GSZ
        keeps = jnp.zeros((1, 1, LANES), jnp.int32)
        for i in range(LANES // GSZ):
            keeps = jnp.where(group == i, retained[h * (LANES // GSZ) + i], keeps)

        def second(kb, carry):
            start = pl.multiple_of(kb * 16, 16)
            block = z[:, pl.ds(start, 16), :]
            pieces = []
            for part in range(2):
                value = block[:, part * 8:part * 8 + 8].reshape(A * 8, LANES)
                high, low = two_parts(value)
                pieces.append(jnp.concatenate([high, high, low], 0))
            value = dot(mid[...], jnp.concatenate(pieces, 1))
            pieces = [value[:, i * LANES:(i + 1) * LANES].reshape(A, 8, LANES) for i in range(2)]
            value = jnp.concatenate(pieces, 1)
            index = start + lax.broadcasted_iota(jnp.int32, (1, 16, LANES), 1)
            value = value * jnp.where(index < keeps, gn[h, :, pl.ds(start, 16), :], 0.0)
            snd[h, :, :, pl.ds(start, 16), :] = value.astype(BF16).reshape(n, jn, 16, LANES)
            return carry

        lax.fori_loop(0, KMAX // 16, second, 0, unroll=2)

    def exchange(src, dst, ssem, rsem, h):
        copies = []
        for s in range(1, n):
            to = lax.rem(me + s, n)
            copies.append(pltpu.make_async_remote_copy(
                src_ref=src.at[h, to], dst_ref=dst.at[h, me],
                send_sem=ssem.at[h, s], recv_sem=rsem.at[h, s],
                device_id={"seq": to}, device_id_type=MESH))
        return copies

    def mix(h):
        rcv[h, me] = snd[h, me]
        if h == 0:
            for i in (2, 3, 4):
                loads["t", i].wait()
        rows = [dg[r:r + 1, h * LANES:(h + 1) * LANES] for r in range(n)]

        def step(i, carry):
            j = i // (KMAX // 16)
            start = pl.multiple_of(lax.rem(i, KMAX // 16) * 16, 16)
            parts = [rcv[h, p, j, pl.ds(start, 16), :].astype(F32) for p in range(n)]
            parts = butterfly(parts, levels)
            parts = [part * row for part, row in zip(parts, rows)]
            parts = butterfly(parts, levels)
            for q in range(n):
                mxo[h, q, j, pl.ds(start, 16), :] = parts[q].astype(BF16)
            return carry

        lax.fori_loop(0, jn * (KMAX // 16), step, 0, unroll=2)
        bck[h, me] = mxo[h, me]

    def inverse_mid(h):
        def step(kb, carry):
            start = pl.multiple_of(kb * 16, 16)
            block = bck[h, :, :, pl.ds(start, 16), :].reshape(A, 16, LANES).astype(F32)
            pieces = [block[:, i * 8:i * 8 + 8].reshape(A * 8, LANES).astype(BF16) for i in range(2)]
            value = jnp.concatenate(pieces, 1)
            value = dot(back[...], jnp.concatenate([value, value], 0))
            for i in range(2):
                part = value[:, i * LANES:(i + 1) * LANES]
                z[:, pl.ds(start + i * 8, 8), :] = part.reshape(A, 8, LANES)
            return carry

        lax.fori_loop(0, KMAX // 16, step, 0, unroll=2)

    def inverse_rows(h, to, skip):
        def step(i, carry):
            a = to * an + skip + i * 2
            high, low = two_parts(jnp.concatenate([z[a], z[a + 1]], 1))
            smooth = dot(inner[...], jnp.concatenate([high, high, low], 0))
            gsd[h, a] = (smooth[:, :LANES] * gt[h, a].astype(F32)).astype(BF16)
            gsd[h, a + 1] = (smooth[:, LANES:] * gt[h, a + 1].astype(F32)).astype(BF16)
            return carry

        lax.fori_loop(0, (an - skip) // 2, step, 0)
        if (an - skip) % 2:
            a = to * an + an - 1
            high, low = two_parts(z[a])
            smooth = dot(inner[...], jnp.concatenate([high, high, low], 0))
            gsd[h, a] = (smooth * gt[h, a].astype(F32)).astype(BF16)

    def run(copies):
        for copy in copies:
            copy.start()

    first = [exchange(snd, rcv, s1, r1, h) for h in range(halves)]
    second = [exchange(mxo, bck, s2, r2, h) for h in range(halves)]
    third = []
    fourth = []
    crossing = [s for level in reversed(range(nc.bit_length() - 1)) for s in range(1 << level, 2 << level)]

    outer = 1 - lax.rem((mc + nc // 4) // (nc // 2), 2)
    order = [s + outer * (i + 1 - s) for i, s in enumerate(crossing)]

    def partner(s):
        to = mc
        for level in range(nc.bit_length() - 1):
            flip = lax.rem(s // (1 << level), 2)
            to = to + flip * ((1 << level) - lax.rem(mc // (1 << level), 2) * (2 << level))
        return to


    def finish(h):
        for copy in second[h]:
            copy.wait_recv()
        inverse_mid(h)
        loads["g", h].wait()
        skip = early if h == 0 else 0
        if h == 0:
            for s in order:
                to = partner(s)
                ysd[pl.ds(to * early, early)] = z[pl.ds(to * an, early)].astype(BF16)
                copy = pltpu.make_async_remote_copy(
                    src_ref=ysd.at[pl.ds(to * early, early)], dst_ref=yrc.at[s],
                    send_sem=s5.at[s], recv_sem=r5.at[s],
                    device_id={"ch": to}, device_id_type=MESH)
                copy.start()
                fourth.append((s, copy))
        for s in order:
            to = partner(s)
            inverse_rows(h, to, skip)
            copy = pltpu.make_async_remote_copy(
                src_ref=gsd.at[h, pl.ds(to * an + skip, an - skip)],
                dst_ref=out.at[h, mc, pl.ds(skip, an - skip)],
                send_sem=s3.at[h, s], recv_sem=r3.at[h, s],
                device_id={"ch": to}, device_id_type=MESH)
            copy.start()
            third.append(copy)
        inverse_rows(h, mc, 0)
        copy = pltpu.make_async_copy(gsd.at[h, pl.ds(mc * an, an)], out.at[h, mc], own3.at[h])
        copy.start()
        third.append(copy)

    pl.semaphore_wait(barrier, n - 1 + nc - 1)
    gates = []
    for s in order:
        to = partner(s)
        copy = pltpu.make_async_remote_copy(
            src_ref=gate.at[pl.ds(to * an, early), :, cut(0)], dst_ref=grc.at[s],
            send_sem=s4.at[s], recv_sem=r4.at[s],
            device_id={"ch": to}, device_id_type=MESH)
        copy.start()
        gates.append(copy)
    forward(0)
    run(first[0])
    for h in range(halves):
        if h + 1 < halves:
            forward(h + 1)
        for copy in first[h]:
            copy.wait_recv()
        mix(h)
        run(second[h])
        if h + 1 < halves:
            run(first[h + 1])
        finish(h)
    stores = []
    for copy in gates:
        copy.wait()
    for s, copy in fourth:
        copy.wait()

        def step(i, carry):
            a = i * 2
            value = jnp.concatenate([yrc[s, a], yrc[s, a + 1]], 1)
            smooth = dot(inner[:, :2 * KMAX], jnp.concatenate([value, value], 0))
            ystage[s, a] = (smooth[:, :LANES] * grc[s, a].astype(F32)).astype(BF16)
            ystage[s, a + 1] = (smooth[:, LANES:] * grc[s, a + 1].astype(F32)).astype(BF16)
            return carry

        lax.fori_loop(0, early // 2, step, 0)
        if early % 2:
            a = early - 1
            value = yrc[s, a]
            smooth = dot(inner[:, :2 * KMAX], jnp.concatenate([value, value], 0))
            ystage[s, a] = (smooth * grc[s, a].astype(F32)).astype(BF16)
        source = partner(s)
        store = pltpu.make_async_copy(ystage.at[s], out.at[0, source, pl.ds(0, early)], own5.at[s])
        store.start()
        stores.append(store)
    for copy in stores + third:
        copy.wait()
    for copies in first + second:
        for copy in copies:
            copy.wait_send()


def mixing_kernel(nc, halves, nb, gathered, weight, mixing, out):
    size = weight.shape[1]
    per = size // LANES
    tiles = [gathered[h, c].reshape(-1, LANES) for c in range(nc) for h in range(halves)]
    sections = [
        dot(jnp.concatenate(tiles[i * per:(i + 1) * per], 1), weight[i]) for i in range(nb)
    ]
    for k in range(nb):
        total = sections[0] * mixing[k, 0:1]
        for i in range(1, nb):
            total += sections[i] * mixing[k, i:i + 1]
        out[:, k * size:(k + 1) * size] = total.astype(BF16)


def local(n, nc, tokens, gating, spectral_gain, device_gain, retained, block_weight, mix_weight):
    rows, width = tokens.shape
    halves = width // LANES
    an = A // nc
    jn = A // n
    early = max(1, an * 5 // 8)
    steps = [jnp.asarray(table) for table in tables()]
    any_space = pl.BlockSpec(memory_space=pl.ANY)
    dma = pltpu.SemaphoreType.DMA
    share = (halves, n, jn, KMAX, LANES)
    gathered = pl.pallas_call(
        functools.partial(filter_kernel, n, nc, halves, early),
        out_shape=jax.ShapeDtypeStruct((halves, nc, an, B, LANES), BF16),
        in_specs=[pl.BlockSpec(memory_space=pltpu.HBM)] * 9,
        out_specs=any_space,
        scratch_shapes=[
            pltpu.VMEM((halves, A, B, LANES), BF16),
            pltpu.VMEM((halves, A, B, LANES), BF16),
            pltpu.VMEM((halves, A, KMAX, LANES), F32),
            pltpu.VMEM((A, KMAX, LANES), F32),
            pltpu.VMEM(share, BF16),
            pltpu.VMEM(share, BF16),
            pltpu.VMEM(share, BF16),
            pltpu.VMEM(share, BF16),
            pltpu.VMEM((halves, A, B, LANES), BF16),
            pltpu.VMEM((nc * early, KMAX, LANES), BF16),
            pltpu.VMEM((nc, early, KMAX, LANES), BF16),
            pltpu.VMEM((nc, early, B, LANES), BF16),
            pltpu.VMEM((nc, early, B, LANES), BF16),
            *[pltpu.VMEM(step.shape, BF16) for step in steps],
            pltpu.VMEM((n, width), F32),
            pltpu.SMEM(retained.shape, jnp.int32),
            dma((6,)),
            dma((halves,)), dma((halves,)), dma((halves,)),
            dma((halves, n)), dma((halves, n)), dma((halves, n)), dma((halves, n)),
            dma((halves, nc)), dma((halves, nc)), dma((halves,)),
            dma((nc,)), dma((nc,)), dma((nc,)), dma((nc,)), dma((nc,)),
        ],
        compiler_params=pltpu.CompilerParams(
            collective_id=0, has_side_effects=True, vmem_limit_bytes=60 * 1024 * 1024),
        name="filter",
    )(tokens.reshape(A, B, width), gating.reshape(A, B, width), spectral_gain, device_gain,
      retained, *steps)
    nb, size, _ = block_weight.shape
    mixing = jnp.transpose(mix_weight, (1, 2, 0))
    step = 4 if an % 4 == 0 else 1
    return pl.pallas_call(
        functools.partial(mixing_kernel, nc, halves, nb),
        out_shape=jax.ShapeDtypeStruct((an * B, nb * size), BF16),
        grid=(an // step,),
        in_specs=[
            pl.BlockSpec((halves, nc, step, B, LANES), lambda i: (0, 0, i, 0, 0)),
            pl.BlockSpec(block_weight.shape, lambda i: (0, 0, 0)),
            pl.BlockSpec(mixing.shape, lambda i: (0, 0, 0)),
        ],
        out_specs=pl.BlockSpec((step * B, nb * size), lambda i: (i, 0)),
        compiler_params=pltpu.CompilerParams(vmem_limit_bytes=60 * 1024 * 1024),
        name="mixing",
    )(gathered, block_weight, mixing)


def solution(mesh):
    in_specs = (
        P("seq", "ch"),
        P("seq", "ch"),
        P(None, None, "ch"),
        P(None, "ch"),
        P("ch"),
        P(),
        P(),
    )
    out_specs = P(("seq", "ch"), None)
    body = functools.partial(local, mesh.shape["seq"], mesh.shape["ch"])
    return jax.shard_map(body, mesh=mesh, in_specs=in_specs, out_specs=out_specs, check_vma=False)
```
